32 devices in a mesh: girth: 4 (over y, x), wall: 8 (over z, core).
Axes of the slice: x: 2, y: 2, z: 4, core: 2. Of those that a mesh axis runs over, the one named last changes fastest.
Arguments:
- adjoint_start: float32 [6, 64, 128, 128], P(None, 'girth', 'wall'), may hold values from -6 to 6
- right_side: float32 [6, 64, 128, 128], P(None, 'girth', 'wall'), may hold values from -6 to 6
- pivot_inverse: bfloat16 [6, 6, 64, 128, 128], P(None, None, 'girth', 'wall'), may hold values from -1.5 to 1.5, as said below
- lower_coupling: bfloat16 [6, 6, 64, 128, 128], P(None, None, 'girth', 'wall'), may hold values from -1 to 1, as said below
- upper_coupling: bfloat16 [6, 6, 64, 128, 128], P(None, None, 'girth', 'wall'), may hold values from -1 to 1, as said below
- girth_coeff: bfloat16 [6, 64, 128, 128], P(None, 'girth', 'wall'), may hold values from 0.0059814453 to 0.023925781
- stream_coeff: bfloat16 [6, 64, 128, 128], P(None, 'girth', 'wall'), may hold values from 0.0029907227 to 0.011962891
Outputs:
- adjoint_out: float32 [6, 64, 128, 128], P(None, 'girth', 'wall')
The draws below stay inside these ranges and needn't reach their ends.
Inputs may be any that keep to these rules, and one draw needn't show every extreme that they name: `pivot_inverse`: one 6 x 6 block for each cell. `lower_coupling`: one 6 x 6 block for each cell. `upper_coupling`: one 6 x 6 block for each cell.
All inputs are finite; a program needn't handle non-finite values.
Results may differ from the reference program's by a relative error of at most 0.0003.
Values sent between devices are 32-bit elements; how exact they have to be, the bound alone decides.
A program may use at most 128 MiB of HBM per device.

```python
import math
import jax
import jax.numpy as jnp
from jax import lax

NV = 6
S = 128
SWEEPS = 2
G = 64
WALL_NORMAL = 128


def line_rates(base_key, upward):
    shared_key = jax.random.fold_in(base_key, 11)
    shuffle_key, carried_key, reach_key = jax.random.split(shared_key, 3)
    shuffled = jax.random.permutation(shuffle_key, NV)
    carried_count = jax.random.randint(carried_key, (), 2, NV - 1)
    carried_up = shuffled < carried_count
    reaches = WALL_NORMAL * jnp.exp(jax.random.uniform(reach_key, (NV,), jnp.float32, jnp.log(0.5), jnp.log(12.0)))
    private_key = jax.random.fold_in(base_key, 21 if upward else 22)
    multiplier_key, brief_rates_key, spike_random_key = jax.random.split(private_key, 3)
    girth_factor = jnp.exp(jax.random.uniform(multiplier_key, (1, G, 1, 1), jnp.float32, jnp.log(0.5), jnp.log(2.0)))
    extended_rates = jnp.exp(-1.0 / (reaches[:, None, None, None] * girth_factor))
    spike_positions = jax.random.randint(spike_random_key, (3,), 0, WALL_NORMAL)
    normal_cell_index = jnp.arange(WALL_NORMAL, dtype=jnp.int32)
    spike_magnitude_scale = jnp.where(jnp.any(normal_cell_index[None, :] == spike_positions[:, None], axis=0), 0.6, 1.0)
    extended_rates = extended_rates * spike_magnitude_scale[None, None, :, None]
    rates_short = jax.random.uniform(brief_rates_key, (NV, G, WALL_NORMAL, S), jnp.float32, 0.3, 0.7)
    carried_here = carried_up if upward else jnp.logical_not(carried_up)
    return jnp.where(carried_here[:, None, None, None], extended_rates, rates_short)


def coupling_block(mixing_key, rates):
    mixing = jax.random.uniform(mixing_key, (NV, NV, G, WALL_NORMAL, S), jnp.float32, -0.08, 0.08)
    identity_block = jnp.eye(NV, dtype=jnp.float32)[:, :, None, None, None]
    return rates[:, None] * (identity_block + (1.0 - identity_block) * mixing)


def draw_lower_coupling(key, part):
    rates = line_rates(key, True)
    return coupling_block(jax.random.fold_in(key, 31), rates).astype(jnp.bfloat16)


def draw_upper_coupling(key, part):
    rates = line_rates(key, False)
    return coupling_block(jax.random.fold_in(key, 32), rates).astype(jnp.bfloat16)


def draw_pivot_inverse(key, part):
    scale_key, mixing_key = jax.random.split(jax.random.fold_in(key, 41))
    lowest, highest, spread_size = (1.0, 4.0, 0.1)
    pivots = jnp.exp(jax.random.uniform(scale_key, (NV, 1, G, WALL_NORMAL, S), jnp.float32, jnp.log(lowest), jnp.log(highest)))
    mixing = jax.random.uniform(mixing_key, (NV, NV, G, WALL_NORMAL, S), jnp.float32, -spread_size, spread_size)
    identity_block = jnp.eye(NV, dtype=jnp.float32)[:, :, None, None, None]
    return ((identity_block + (1.0 - identity_block) * mixing) / pivots).astype(jnp.bfloat16)


def shard_levels(own_key, extent, cuts, smallest, largest):
    factor_of = 1.0
    for dim, blocks in cuts:
        draws = jax.random.uniform(jax.random.fold_in(jax.random.fold_in(own_key, 6), dim), (blocks,), jnp.float32, smallest / len(cuts), largest / len(cuts))
        factor_of = factor_of * jnp.repeat(jnp.exp(draws), extent[dim] // blocks).reshape((-1,) + (1,) * (len(extent) - 1 - dim))
    return factor_of


def noise(stream_key, extent, spread, bound, shards=(), held_as=jnp.bfloat16):
    entries = jax.random.normal(stream_key, extent, jnp.float32) * spread
    if len(shards) > 0:
        entries = shard_levels(stream_key, extent, shards, -0.22, 0.18) * entries
    return jnp.clip(entries, min=-bound, max=bound).astype(held_as)


def setup_inputs(seed: int = 0) -> dict:
    key_of = jax.random.split(jax.random.key(seed), 8)
    adjoint_start = noise(key_of[0], (NV, G, WALL_NORMAL, S), 1.0, 6.0, ((1, 4), (2, 8)), jnp.float32)
    right_side = noise(key_of[1], (NV, G, WALL_NORMAL, S), 1.0, 6.0, ((1, 4), (2, 8)), jnp.float32)
    pivot_inverse = draw_pivot_inverse(jax.random.fold_in(key_of[7], 71), 0)
    lower_coupling = draw_lower_coupling(jax.random.fold_in(key_of[7], 71), 0)
    upper_coupling = draw_upper_coupling(jax.random.fold_in(key_of[7], 71), 0)
    girth_coeff = jnp.clip(jnp.exp(math.log(0.023925781) - 1.3862944 * jax.random.uniform(key_of[5], (NV, G, WALL_NORMAL, S), jnp.float32) ** shard_levels(key_of[5], (NV, G, WALL_NORMAL, S), ((1, 4), (2, 8)), -0.2, 0.2)), 0.0059814453, 0.023925781).astype(jnp.bfloat16)
    stream_coeff = jnp.clip(jnp.exp(math.log(0.011962891) - 1.3862944 * jax.random.uniform(key_of[6], (NV, G, WALL_NORMAL, S), jnp.float32) ** shard_levels(key_of[6], (NV, G, WALL_NORMAL, S), ((1, 4), (2, 8)), -0.2, 0.2)), 0.0029907227, 0.011962891).astype(jnp.bfloat16)
    return {"adjoint_start": adjoint_start, "right_side": right_side, "pivot_inverse": pivot_inverse, "lower_coupling": lower_coupling, "upper_coupling": upper_coupling, "girth_coeff": girth_coeff, "stream_coeff": stream_coeff}


def apply_blocks(blocks, vectors):
    return jnp.sum(blocks.astype(jnp.float32) * vectors[None], axis=1)


def neighbour_term(adjoint, girth_coeff, stream_coeff):
    beside_pair = jnp.roll(adjoint, 1, axis=1) + jnp.roll(adjoint, -1, axis=1)
    distant_pair = jnp.roll(adjoint, 2, axis=1) + jnp.roll(adjoint, -2, axis=1)
    padded = jnp.pad(adjoint, ((0, 0), (0, 0), (0, 0), (1, 1)))
    streamwise = padded[..., :-2] + padded[..., 2:]
    return girth_coeff.astype(jnp.float32) * (beside_pair - 0.25 * distant_pair) + stream_coeff.astype(jnp.float32) * streamwise


def take_layer(values, wall_step):
    return lax.dynamic_index_in_dim(values, wall_step, values.ndim - 2, False)


def relax(adjoint, right_side, pivot_inverse, lower_coupling, upper_coupling, girth_coeff, stream_coeff):
    wall_cells = adjoint.shape[2]
    loaded = right_side + neighbour_term(adjoint, girth_coeff, stream_coeff)
    zero_layer = jnp.zeros_like(adjoint[:, :, :1])
    raised = jnp.concatenate([adjoint[:, :, 1:], zero_layer], axis=2)
    start_value = jnp.zeros_like(adjoint[:, :, 0])
    steps_order = jnp.arange(wall_cells, dtype=jnp.int32)

    def forward_step(carried, wall_step):
        lifted_prev, solved_prev = carried
        lifted = take_layer(adjoint, wall_step) - apply_blocks(take_layer(upper_coupling, wall_step), take_layer(raised, wall_step))
        lower_blocks = take_layer(lower_coupling, wall_step)
        source = apply_blocks(take_layer(pivot_inverse, wall_step), take_layer(loaded, wall_step)) - (lifted - apply_blocks(lower_blocks, lifted_prev))
        solved = source + apply_blocks(lower_blocks, solved_prev)
        return (lifted, solved), solved

    unused, forward_values = lax.scan(forward_step, (start_value, start_value), steps_order)

    def backward_step(solved_next, inputs):
        wall_step, forward_value = inputs
        solved = forward_value + apply_blocks(take_layer(upper_coupling, wall_step), solved_next)
        return solved, solved

    unused_last, backward_values = lax.scan(backward_step, start_value, (steps_order, forward_values), reverse=True)
    return adjoint + jnp.moveaxis(backward_values, 0, 2)


def reference(adjoint_start, right_side, pivot_inverse, lower_coupling, upper_coupling, girth_coeff, stream_coeff):
    adjoint = adjoint_start
    for repeat in range(SWEEPS):
        adjoint = relax(adjoint, right_side, pivot_inverse, lower_coupling, upper_coupling, girth_coeff, stream_coeff)
    return adjoint
```

```python
import functools

import jax
import jax.numpy as jnp
from jax import lax
from jax.experimental import pallas as pl
from jax.experimental.pallas import tpu as pltpu
from jax.sharding import PartitionSpec as P

SWEEPS = 2
HALO = 2
HALVES = 2
MESH = pl.DeviceIdType.MESH
F32 = jnp.float32


def block_product(column, vector):
    total = column(0) * vector[0][None]
    for j in range(1, vector.shape[0]):
        total = total + column(j) * vector[j][None]
    return total


def kernel(
    girth_size,
    wall_size,
    sizes,
    adj_hbm,
    rhs_hbm,
    piv_hbm,
    low_hbm,
    upp_hbm,
    gc_hbm,
    sc_hbm,
    out_ref,
    adj,
    rhs,
    piv,
    low,
    upp,
    gc,
    sc,
    couplings,
    work,
    own_map,
    pair_map,
    chip_map,
    own_tip,
    pair_tip,
    chip_tip,
    entering,
    start_tip,
    load_sem,
    halo_send,
    halo_recv,
    map_send,
    map_recv,
    tip_send,
    tip_recv,
    chain_send,
    chain_recv,
):
    nv, girth, wall, stream = sizes
    half = girth // HALVES
    chips = wall_size // 2
    my_girth = lax.axis_index("girth")
    my_wall = lax.axis_index("wall")
    chip = my_wall // 2
    core = lax.rem(my_wall, 2)
    right = (lax.rem(my_girth + 1, girth_size), my_wall)
    left = (lax.rem(my_girth + girth_size - 1, girth_size), my_wall)
    partner = (my_girth, chip * 2 + 1 - core)

    def on_chip(other_chip, other_core):
        return (my_girth, other_chip * 2 + other_core)

    body_rows = pl.ds(HALO * wall, girth * wall)
    loads = [
        pltpu.make_async_copy(adj_hbm, adj.at[0, :, body_rows, :], load_sem.at[0]),
        pltpu.make_async_copy(low_hbm, low, load_sem.at[1]),
        pltpu.make_async_copy(rhs_hbm, rhs, load_sem.at[2]),
        pltpu.make_async_copy(gc_hbm, gc, load_sem.at[3]),
        pltpu.make_async_copy(sc_hbm, sc, load_sem.at[4]),
        pltpu.make_async_copy(piv_hbm, piv, load_sem.at[5]),
        pltpu.make_async_copy(upp_hbm, upp, load_sem.at[6]),
    ]
    for load in loads:
        load.start()

    barrier = pltpu.get_barrier_semaphore()

    def greet(device):
        pl.semaphore_signal(barrier, inc=1, device_id=device, device_id_type=MESH)

    greet(left)
    greet(right)
    greet(partner)

    @pl.when(chip > 0)
    def _():
        greet(on_chip(chip - 1, core))

        @pl.when(core == 0)
        def _():
            greet(on_chip(chip - 1, 1))

    @pl.when(chip < chips - 1)
    def _():
        greet(on_chip(chip + 1, core))

        @pl.when(core == 1)
        def _():
            greet(on_chip(chip + 1, 0))

    from_below = jnp.where(chip > 0, 2 - core, 0)
    from_above = jnp.where(chip < chips - 1, 1 + core, 0)
    pl.semaphore_wait(barrier, 3 + from_below + from_above)

    def remote(src, dst, send_sem, recv_sem, device):
        return pltpu.make_async_remote_copy(
            src_ref=src,
            dst_ref=dst,
            send_sem=send_sem,
            recv_sem=recv_sem,
            device_id=device,
            device_id_type=MESH,
        )

    def halo_copies(sweep):
        field = adj.at[sweep]
        width = HALO * wall
        return [
            remote(
                field.at[:, pl.ds(width, width), :],
                field.at[:, pl.ds(width + girth * wall, width), :],
                halo_send.at[sweep, 0],
                halo_recv.at[sweep, 0],
                left,
            ),
            remote(
                field.at[:, pl.ds(girth * wall, width), :],
                field.at[:, pl.ds(0, width), :],
                halo_send.at[sweep, 1],
                halo_recv.at[sweep, 1],
                right,
            ),
        ]

    def layer(w):
        return pl.ds(pl.multiple_of(w * girth, girth), girth)

    def coupling_column(d, w):
        return lambda j: couplings[d, :, j, layer(w), :]

    def order(d, step):
        return step if d == 0 else wall - 1 - step

    def transpose_coupling(d, source):
        def one_girth(g, carry):
            couplings[d, :, :, pl.ds(g, wall, stride=girth), :] = source[:, :, g].astype(F32)
            return carry

        lax.fori_loop(0, girth, one_girth, 0)

    def map_copy(d):
        return remote(own_map.at[d], pair_map.at[d], map_send.at[d], map_recv.at[d], partner)

    def make_map(d):
        for k in range(0, nv, 2):

            def advance(step, columns):
                column = coupling_column(d, order(d, step))
                return tuple(block_product(column, c) for c in columns)

            first = coupling_column(d, order(d, 0))
            columns = lax.fori_loop(1, wall, advance, (first(k), first(k + 1)))
            own_map[d, :, k] = columns[0]
            own_map[d, :, k + 1] = columns[1]

        @pl.when(core == d)
        def _():
            map_copy(d).start()

    def make_chip_map(d):
        @pl.when(core != d)
        def _():
            map_copy(d).wait_recv()

            def one_column(k, carry):
                chip_map[d, :, k] = block_product(
                    lambda j: own_map[d, :, j], pair_map[d, :, k]
                )
                return carry

            lax.fori_loop(0, nv, one_column, 0)

    lane = lax.broadcasted_iota(jnp.int32, (nv, wall, stream), 2)

    def make_source(sweep, g):
        def girth_layer(offset):
            rows = pl.ds(pl.multiple_of((g + HALO + offset) * wall, wall), wall)
            return adj[sweep, :, rows, :]

        here = girth_layer(0)
        beside_pair = girth_layer(-1) + girth_layer(1)
        distant_pair = girth_layer(-2) + girth_layer(2)
        before = jnp.where(lane == 0, 0.0, pltpu.roll(here, 1, 2))
        after = jnp.where(lane == stream - 1, 0.0, pltpu.roll(here, stream - 1, 2))
        neighbours = gc[:, g].astype(F32) * (beside_pair - 0.25 * distant_pair) + sc[
            :, g
        ].astype(F32) * (before + after)
        loaded = rhs[:, g] + neighbours
        work[:, pl.ds(g, wall, stride=girth), :] = block_product(
            lambda j: piv[:, j, g].astype(F32), loaded
        )

    def make_sources(sweep):
        def body(g, carry):
            make_source(sweep, g)
            return carry

        lax.fori_loop(HALO, girth - HALO, body, 0)
        for copy in halo_copies(sweep):
            copy.wait_recv()
        lax.fori_loop(0, HALO, body, 0)
        lax.fori_loop(girth - HALO, girth, body, 0)

    def advance_line(d, step, vector):
        w = order(d, step)
        return w, work[:, layer(w), :] + block_product(coupling_column(d, w), vector)

    def find_tip(sweep, d):
        first = work[:, layer(order(d, 0)), :]
        tip = lax.fori_loop(1, wall, lambda step, v: advance_line(d, step, v)[1], first)
        for h in range(HALVES):
            own_tip[sweep, d, h] = tip[:, h * half : (h + 1) * half]

    def rows_of(h):
        return pl.ds(h * half, half)

    def tip_copy(sweep, d, h):
        return remote(
            own_tip.at[sweep, d, h],
            pair_tip.at[sweep, d, h],
            tip_send.at[sweep, d, h],
            tip_recv.at[sweep, d, h],
            partner,
        )

    def chain_copy(sweep, d, h, target_core):
        next_chip = chip + 1 if d == 0 else chip - 1
        return remote(
            chip_tip.at[sweep, d, h],
            entering.at[sweep, d, h],
            chain_send.at[sweep, d, h, target_core],
            chain_recv.at[sweep, d, h],
            on_chip(next_chip, target_core),
        )

    def has_previous(d):
        return chip > 0 if d == 0 else chip < chips - 1

    def has_next(d):
        return chip < chips - 1 if d == 0 else chip > 0

    def send_tips(sweep, d):
        @pl.when(core == d)
        def _():
            for h in range(HALVES):
                tip_copy(sweep, d, h).start()

    def run_chain(sweep, d):
        @pl.when(core != d)
        def _():
            for h in range(HALVES):
                tip_copy(sweep, d, h).wait_recv()
                chip_tip[sweep, d, h] = own_tip[sweep, d, h] + block_product(
                    lambda j: own_map[d, :, j, rows_of(h), :], pair_tip[sweep, d, h]
                )

        @pl.when(jnp.logical_not(has_previous(d)))
        def _():
            entering[sweep, d] = jnp.zeros_like(entering[sweep, d])

        for h in range(HALVES):

            @pl.when(has_previous(d))
            def _():
                chain_copy(sweep, d, h, d).wait_recv()

            @pl.when(jnp.logical_and(core != d, has_next(d)))
            def _():
                chip_tip[sweep, d, h] = chip_tip[sweep, d, h] + block_product(
                    lambda j: chip_map[d, :, j, rows_of(h), :], entering[sweep, d, h]
                )
                chain_copy(sweep, d, h, 1 - d).start()
                chain_copy(sweep, d, h, d).start()

        for h in range(HALVES):

            @pl.when(core == d)
            def _():
                start_tip[:, rows_of(h), :] = entering[sweep, d, h]

            @pl.when(core != d)
            def _():
                start_tip[:, rows_of(h), :] = pair_tip[sweep, d, h] + block_product(
                    lambda j: pair_map[d, :, j, rows_of(h), :], entering[sweep, d, h]
                )

    def solve_forward():
        def body(step, vector):
            w, vector = advance_line(0, step, vector)
            work[:, layer(w), :] = vector
            return vector

        lax.fori_loop(0, wall, body, start_tip[...])

    def solve_backward(store):
        def body(step, vector):
            w, vector = advance_line(1, step, vector)
            store(w, vector)
            return vector

        lax.fori_loop(0, wall, body, start_tip[...])

    loads[0].wait()
    for copy in halo_copies(0):
        copy.start()
    loads[1].wait()
    transpose_coupling(0, low)
    make_map(0)
    for load in loads[2:6]:
        load.wait()

    for sweep in range(SWEEPS):
        make_sources(sweep)
        find_tip(sweep, 0)
        send_tips(sweep, 0)
        if sweep == 0:
            make_chip_map(0)
            loads[6].wait()
            transpose_coupling(1, upp)
            make_map(1)
        run_chain(sweep, 0)
        solve_forward()
        find_tip(sweep, 1)
        send_tips(sweep, 1)
        if sweep == 0:
            make_chip_map(1)
        run_chain(sweep, 1)
        if sweep < SWEEPS - 1:

            def store(w, vector):
                adj[sweep + 1, :, pl.ds(HALO * wall + w, girth, stride=wall), :] = vector

            solve_backward(store)
            for copy in halo_copies(sweep + 1):
                copy.start()
        else:

            def store(w, vector):
                out_ref[:, pl.ds(w, girth, stride=wall), :] = vector

            solve_backward(store)

    for sweep in range(SWEEPS):
        for copy in halo_copies(sweep):
            copy.wait_send()
    for d in range(2):

        @pl.when(core == d)
        def _():
            map_copy(d).wait_send()
            for sweep in range(SWEEPS):
                for h in range(HALVES):
                    tip_copy(sweep, d, h).wait_send()

        @pl.when(jnp.logical_and(core != d, has_next(d)))
        def _():
            for sweep in range(SWEEPS):
                for h in range(HALVES):
                    chain_copy(sweep, d, h, 0).wait_send()
                    chain_copy(sweep, d, h, 1).wait_send()


def on_device(
    girth_size,
    wall_size,
    adjoint_start,
    right_side,
    pivot_inverse,
    lower_coupling,
    upper_coupling,
    girth_coeff,
    stream_coeff,
):
    nv, girth, wall, stream = adjoint_start.shape
    half = girth // HALVES
    flat = (nv, girth * wall, stream)
    blocks = (nv, nv, girth, wall, stream)
    tips = (SWEEPS, 2, HALVES, nv, half, stream)
    maps = (2, nv, nv, girth, stream)
    dma = pltpu.SemaphoreType.DMA
    out = pl.pallas_call(
        functools.partial(kernel, girth_size, wall_size, (nv, girth, wall, stream)),
        out_shape=jax.ShapeDtypeStruct(flat, F32),
        in_specs=[pl.BlockSpec(memory_space=pl.ANY)] * 7,
        out_specs=pl.BlockSpec(memory_space=pltpu.VMEM),
        scratch_shapes=[
            pltpu.VMEM((SWEEPS, nv, (girth + 2 * HALO) * wall, stream), F32),
            pltpu.VMEM((nv, girth, wall, stream), F32),
            pltpu.VMEM(blocks, jnp.bfloat16),
            pltpu.VMEM(blocks, jnp.bfloat16),
            pltpu.VMEM(blocks, jnp.bfloat16),
            pltpu.VMEM((nv, girth, wall, stream), jnp.bfloat16),
            pltpu.VMEM((nv, girth, wall, stream), jnp.bfloat16),
            pltpu.VMEM((2, nv, nv, wall * girth, stream), F32),
            pltpu.VMEM((nv, wall * girth, stream), F32),
            pltpu.VMEM(maps, F32),
            pltpu.VMEM(maps, F32),
            pltpu.VMEM(maps, F32),
            pltpu.VMEM(tips, F32),
            pltpu.VMEM(tips, F32),
            pltpu.VMEM(tips, F32),
            pltpu.VMEM(tips, F32),
            pltpu.VMEM((nv, girth, stream), F32),
            dma((7,)),
            dma((SWEEPS, 2)),
            dma((SWEEPS, 2)),
            dma((2,)),
            dma((2,)),
            dma((SWEEPS, 2, HALVES)),
            dma((SWEEPS, 2, HALVES)),
            dma((SWEEPS, 2, HALVES, 2)),
            dma((SWEEPS, 2, HALVES)),
        ],
        compiler_params=pltpu.CompilerParams(
            collective_id=0, has_side_effects=True, vmem_limit_bytes=48 * 2**20
        ),
    )(
        adjoint_start.reshape(flat),
        right_side,
        pivot_inverse,
        lower_coupling,
        upper_coupling,
        girth_coeff,
        stream_coeff,
    )
    return out.reshape(adjoint_start.shape)


def solution(mesh):
    in_specs = (
        P(None, "girth", "wall", None),
        P(None, "girth", "wall", None),
        P(None, None, "girth", "wall", None),
        P(None, None, "girth", "wall", None),
        P(None, None, "girth", "wall", None),
        P(None, "girth", "wall", None),
        P(None, "girth", "wall", None),
    )
    out_specs = P(None, "girth", "wall", None)
    return jax.shard_map(
        functools.partial(on_device, mesh.shape["girth"], mesh.shape["wall"]),
        mesh=mesh,
        in_specs=in_specs,
        out_specs=out_specs,
        check_vma=False,
    )
```

```python
import functools

import jax
import jax.numpy as jnp
from jax import lax
from jax.experimental import pallas as pl
from jax.experimental.pallas import tpu as pltpu
from jax.sharding import PartitionSpec as P

SWEEPS = 2
HALO = 2
HALVES = 2
MESH = pl.DeviceIdType.MESH
F32 = jnp.float32


def block_product(column, vector):
    total = column(0) * vector[0][None]
    for j in range(1, vector.shape[0]):
        total = total + column(j) * vector[j][None]
    return total


def kernel(
    girth_size,
    wall_size,
    sizes,
    adj_hbm,
    rhs_hbm,
    piv_hbm,
    low_hbm,
    upp_hbm,
    gc_hbm,
    sc_hbm,
    out_ref,
    adj,
    rhs,
    piv,
    low,
    upp,
    gc,
    sc,
    couplings,
    work,
    staged,
    own_map,
    pair_map,
    chip_map,
    own_tip,
    pair_tip,
    chip_tip,
    entering,
    start_tip,
    load_sem,
    halo_send,
    halo_recv,
    map_send,
    map_recv,
    tip_send,
    tip_recv,
    chain_send,
    chain_recv,
):
    nv, girth, wall, stream = sizes
    half = girth // HALVES
    chips = wall_size // 2
    my_girth = lax.axis_index("girth")
    my_wall = lax.axis_index("wall")
    chip = my_wall // 2
    core = lax.rem(my_wall, 2)
    right = (lax.rem(my_girth + 1, girth_size), my_wall)
    left = (lax.rem(my_girth + girth_size - 1, girth_size), my_wall)
    partner = (my_girth, chip * 2 + 1 - core)

    def on_chip(other_chip, other_core):
        return (my_girth, other_chip * 2 + other_core)

    body_rows = pl.ds(HALO * wall, girth * wall)
    loads = [
        pltpu.make_async_copy(adj_hbm, adj.at[0, :, body_rows, :], load_sem.at[0]),
        pltpu.make_async_copy(low_hbm, low, load_sem.at[1]),
        pltpu.make_async_copy(rhs_hbm, rhs, load_sem.at[2]),
        pltpu.make_async_copy(gc_hbm, gc, load_sem.at[3]),
        pltpu.make_async_copy(sc_hbm, sc, load_sem.at[4]),
        pltpu.make_async_copy(piv_hbm, piv, load_sem.at[5]),
        pltpu.make_async_copy(upp_hbm, upp, load_sem.at[6]),
    ]
    for load in loads:
        load.start()

    barrier = pltpu.get_barrier_semaphore()

    def greet(device):
        pl.semaphore_signal(barrier, inc=1, device_id=device, device_id_type=MESH)

    greet(left)
    greet(right)
    greet(partner)

    @pl.when(chip > 0)
    def _():
        greet(on_chip(chip - 1, core))

        @pl.when(core == 0)
        def _():
            greet(on_chip(chip - 1, 1))

    @pl.when(chip < chips - 1)
    def _():
        greet(on_chip(chip + 1, core))

        @pl.when(core == 1)
        def _():
            greet(on_chip(chip + 1, 0))

    from_below = jnp.where(chip > 0, 2 - core, 0)
    from_above = jnp.where(chip < chips - 1, 1 + core, 0)

    def remote(src, dst, send_sem, recv_sem, device):
        return pltpu.make_async_remote_copy(
            src_ref=src,
            dst_ref=dst,
            send_sem=send_sem,
            recv_sem=recv_sem,
            device_id=device,
            device_id_type=MESH,
        )

    def halo_copies(sweep):
        field = adj.at[sweep]
        width = HALO * wall
        return [
            remote(
                field.at[:, pl.ds(width, width), :],
                field.at[:, pl.ds(width + girth * wall, width), :],
                halo_send.at[sweep, 0],
                halo_recv.at[sweep, 0],
                left,
            ),
            remote(
                field.at[:, pl.ds(girth * wall, width), :],
                field.at[:, pl.ds(0, width), :],
                halo_send.at[sweep, 1],
                halo_recv.at[sweep, 1],
                right,
            ),
        ]

    def coupling_column(d, w):
        return lambda j: couplings[d, :, j, w]

    def order(d, step):
        return step if d == 0 else wall - 1 - step

    def transpose_coupling(d, source):
        def one_row(i, carry):
            for j in range(nv):
                couplings[d, i, j] = jnp.swapaxes(source[i, j].astype(F32), 0, 1)
            return carry

        lax.fori_loop(0, nv, one_row, 0)

    def map_copy(d):
        return remote(own_map.at[d], pair_map.at[d], map_send.at[d], map_recv.at[d], partner)

    def make_map(d):
        for k in range(0, nv, 2):

            def advance(step, columns):
                column = coupling_column(d, order(d, step))
                return tuple(block_product(column, c) for c in columns)

            first = coupling_column(d, order(d, 0))
            columns = lax.fori_loop(1, wall, advance, (first(k), first(k + 1)))
            own_map[d, :, k] = columns[0]
            own_map[d, :, k + 1] = columns[1]

        @pl.when(core == d)
        def _():
            map_copy(d).start()

    def make_chip_map(d):
        @pl.when(core != d)
        def _():
            map_copy(d).wait_recv()

            def one_column(k, carry):
                chip_map[d, :, k] = block_product(
                    lambda j: own_map[d, :, j], pair_map[d, :, k]
                )
                return carry

            lax.fori_loop(0, nv, one_column, 0)

    lane = lax.broadcasted_iota(jnp.int32, (nv, wall, stream), 2)

    def make_source(sweep, g):
        def girth_layer(offset):
            rows = pl.ds(pl.multiple_of((g + HALO + offset) * wall, wall), wall)
            return adj[sweep, :, rows, :]

        here = girth_layer(0)
        beside_pair = girth_layer(-1) + girth_layer(1)
        distant_pair = girth_layer(-2) + girth_layer(2)
        before = jnp.where(lane == 0, 0.0, pltpu.roll(here, 1, 2))
        after = jnp.where(lane == stream - 1, 0.0, pltpu.roll(here, stream - 1, 2))
        neighbours = gc[:, g].astype(F32) * (beside_pair - 0.25 * distant_pair) + sc[
            :, g
        ].astype(F32) * (before + after)
        loaded = rhs[:, g] + neighbours
        staged[:, g] = block_product(
            lambda j: piv[:, j, g].astype(F32), loaded
        )

    def make_sources(sweep):
        def body(g, carry):
            make_source(sweep, g)
            return carry

        lax.fori_loop(HALO, girth - HALO, body, 0)
        for copy in halo_copies(sweep):
            copy.wait_recv()
        lax.fori_loop(0, HALO, body, 0)
        lax.fori_loop(girth - HALO, girth, body, 0)

        def one_variable(i, carry):
            work[i] = jnp.swapaxes(staged[i], 0, 1)
            return carry

        lax.fori_loop(0, nv, one_variable, 0)

    def advance_line(d, step, vector):
        w = order(d, step)
        return w, work[:, w] + block_product(coupling_column(d, w), vector)

    def find_tip(sweep, d):
        first = work[:, order(d, 0)]
        tip = lax.fori_loop(1, wall, lambda step, v: advance_line(d, step, v)[1], first)
        for h in range(HALVES):
            own_tip[sweep, d, h] = tip[:, h * half : (h + 1) * half]

    def rows_of(h):
        return pl.ds(h * half, half)

    def tip_copy(sweep, d, h):
        return remote(
            own_tip.at[sweep, d, h],
            pair_tip.at[sweep, d, h],
            tip_send.at[sweep, d, h],
            tip_recv.at[sweep, d, h],
            partner,
        )

    def chain_copy(sweep, d, h, target_core):
        next_chip = chip + 1 if d == 0 else chip - 1
        return remote(
            chip_tip.at[sweep, d, h],
            entering.at[sweep, d, h],
            chain_send.at[sweep, d, h, target_core],
            chain_recv.at[sweep, d, h],
            on_chip(next_chip, target_core),
        )

    def has_previous(d):
        return chip > 0 if d == 0 else chip < chips - 1

    def has_next(d):
        return chip < chips - 1 if d == 0 else chip > 0

    def send_tips(sweep, d):
        @pl.when(core == d)
        def _():
            for h in range(HALVES):
                tip_copy(sweep, d, h).start()

    def run_chain(sweep, d):
        @pl.when(core != d)
        def _():
            for h in range(HALVES):
                tip_copy(sweep, d, h).wait_recv()
                chip_tip[sweep, d, h] = own_tip[sweep, d, h] + block_product(
                    lambda j: own_map[d, :, j, rows_of(h), :], pair_tip[sweep, d, h]
                )

        @pl.when(jnp.logical_not(has_previous(d)))
        def _():
            entering[sweep, d] = jnp.zeros_like(entering[sweep, d])

        for h in range(HALVES):

            @pl.when(has_previous(d))
            def _():
                chain_copy(sweep, d, h, d).wait_recv()

            @pl.when(jnp.logical_and(core != d, has_next(d)))
            def _():
                chip_tip[sweep, d, h] = chip_tip[sweep, d, h] + block_product(
                    lambda j: chip_map[d, :, j, rows_of(h), :], entering[sweep, d, h]
                )
                chain_copy(sweep, d, h, 1 - d).start()
                chain_copy(sweep, d, h, d).start()

        for h in range(HALVES):

            @pl.when(core == d)
            def _():
                start_tip[:, rows_of(h), :] = entering[sweep, d, h]

            @pl.when(core != d)
            def _():
                start_tip[:, rows_of(h), :] = pair_tip[sweep, d, h] + block_product(
                    lambda j: pair_map[d, :, j, rows_of(h), :], entering[sweep, d, h]
                )

    def solve(d):
        def body(step, vector):
            w, vector = advance_line(d, step, vector)
            work[:, w] = vector
            return vector

        lax.fori_loop(0, wall, body, start_tip[...])

    def prepare_upper():
        loads[6].wait()
        transpose_coupling(1, upp)
        make_map(1)

    in_lower_half = chip < chips // 2

    loads[1].wait()
    transpose_coupling(0, low)
    pl.semaphore_wait(barrier, 3 + from_below + from_above)
    loads[0].wait()
    for copy in halo_copies(0):
        copy.start()
    make_map(0)
    for load in loads[2:6]:
        load.wait()

    for sweep in range(SWEEPS):
        make_sources(sweep)
        find_tip(sweep, 0)
        send_tips(sweep, 0)
        if sweep == 0:
            make_chip_map(0)
            pl.when(jnp.logical_not(in_lower_half))(prepare_upper)
        run_chain(sweep, 0)
        solve(0)
        if sweep == 0:
            pl.when(in_lower_half)(prepare_upper)
        find_tip(sweep, 1)
        send_tips(sweep, 1)
        if sweep == 0:
            make_chip_map(1)
        run_chain(sweep, 1)
        solve(1)
        last = sweep == SWEEPS - 1

        def one_variable(i, carry):
            values = jnp.swapaxes(work[i], 0, 1)
            if last:
                out_ref[i] = values
            else:
                adj[sweep + 1, i, body_rows] = values.reshape(girth * wall, stream)
            return carry

        lax.fori_loop(0, nv, one_variable, 0)
        if not last:
            for copy in halo_copies(sweep + 1):
                copy.start()

    for sweep in range(SWEEPS):
        for copy in halo_copies(sweep):
            copy.wait_send()
    for d in range(2):

        @pl.when(core == d)
        def _():
            map_copy(d).wait_send()
            for sweep in range(SWEEPS):
                for h in range(HALVES):
                    tip_copy(sweep, d, h).wait_send()

        @pl.when(jnp.logical_and(core != d, has_next(d)))
        def _():
            for sweep in range(SWEEPS):
                for h in range(HALVES):
                    chain_copy(sweep, d, h, 0).wait_send()
                    chain_copy(sweep, d, h, 1).wait_send()


def on_device(
    girth_size,
    wall_size,
    adjoint_start,
    right_side,
    pivot_inverse,
    lower_coupling,
    upper_coupling,
    girth_coeff,
    stream_coeff,
):
    nv, girth, wall, stream = adjoint_start.shape
    half = girth // HALVES
    flat = (nv, girth * wall, stream)
    blocks = (nv, nv, girth, wall, stream)
    tips = (SWEEPS, 2, HALVES, nv, half, stream)
    maps = (2, nv, nv, girth, stream)
    dma = pltpu.SemaphoreType.DMA
    out = pl.pallas_call(
        functools.partial(kernel, girth_size, wall_size, (nv, girth, wall, stream)),
        out_shape=jax.ShapeDtypeStruct((nv, girth, wall, stream), F32),
        in_specs=[pl.BlockSpec(memory_space=pl.ANY)] * 7,
        out_specs=pl.BlockSpec(memory_space=pltpu.VMEM),
        scratch_shapes=[
            pltpu.VMEM((SWEEPS, nv, (girth + 2 * HALO) * wall, stream), F32),
            pltpu.VMEM((nv, girth, wall, stream), F32),
            pltpu.VMEM(blocks, jnp.bfloat16),
            pltpu.VMEM(blocks, jnp.bfloat16),
            pltpu.VMEM(blocks, jnp.bfloat16),
            pltpu.VMEM((nv, girth, wall, stream), jnp.bfloat16),
            pltpu.VMEM((nv, girth, wall, stream), jnp.bfloat16),
            pltpu.VMEM((2, nv, nv, wall, girth, stream), F32),
            pltpu.VMEM((nv, wall, girth, stream), F32),
            pltpu.VMEM((nv, girth, wall, stream), F32),
            pltpu.VMEM(maps, F32),
            pltpu.VMEM(maps, F32),
            pltpu.VMEM(maps, F32),
            pltpu.VMEM(tips, F32),
            pltpu.VMEM(tips, F32),
            pltpu.VMEM(tips, F32),
            pltpu.VMEM(tips, F32),
            pltpu.VMEM((nv, girth, stream), F32),
            dma((7,)),
            dma((SWEEPS, 2)),
            dma((SWEEPS, 2)),
            dma((2,)),
            dma((2,)),
            dma((SWEEPS, 2, HALVES)),
            dma((SWEEPS, 2, HALVES)),
            dma((SWEEPS, 2, HALVES, 2)),
            dma((SWEEPS, 2, HALVES)),
        ],
        compiler_params=pltpu.CompilerParams(
            collective_id=0, has_side_effects=True, vmem_limit_bytes=62 * 2**20
        ),
    )(
        adjoint_start.reshape(flat),
        right_side,
        pivot_inverse,
        lower_coupling,
        upper_coupling,
        girth_coeff,
        stream_coeff,
    )
    return out


def solution(mesh):
    in_specs = (
        P(None, "girth", "wall", None),
        P(None, "girth", "wall", None),
        P(None, None, "girth", "wall", None),
        P(None, None, "girth", "wall", None),
        P(None, None, "girth", "wall", None),
        P(None, "girth", "wall", None),
        P(None, "girth", "wall", None),
    )
    out_specs = P(None, "girth", "wall", None)
    return jax.shard_map(
        functools.partial(on_device, mesh.shape["girth"], mesh.shape["wall"]),
        mesh=mesh,
        in_specs=in_specs,
        out_specs=out_specs,
        check_vma=False,
    )
```

```python
import functools

import jax
import jax.numpy as jnp
from jax import lax
from jax.experimental import pallas as pl
from jax.experimental.pallas import tpu as pltpu
from jax.sharding import PartitionSpec as P

SWEEPS = 2
HALO = 2
HALVES = 2
MESH = pl.DeviceIdType.MESH
F32 = jnp.float32


def block_product(column, vector):
    total = column(0) * vector[0][None]
    for j in range(1, vector.shape[0]):
        total = total + column(j) * vector[j][None]
    return total


def kernel(
    girth_size,
    wall_size,
    sizes,
    adj_hbm,
    rhs_hbm,
    piv_hbm,
    low_hbm,
    upp_hbm,
    gc_hbm,
    sc_hbm,
    out_ref,
    adj,
    rhs,
    piv,
    low,
    upp,
    gc,
    sc,
    couplings,
    work,
    staged,
    other_map,
    half_map,
    lead_map,
    other_tip,
    half_tip,
    lead_tip,
    pair_out,
    entering,
    starts,
    other_start,
    start_tip,
    whole_column,
    load_sem,
    halo_send,
    halo_recv,
    map_send,
    map_recv,
    lead_map_send,
    lead_map_recv,
    tip_send,
    tip_recv,
    lead_send,
    lead_recv,
    pair_send,
    pair_recv,
    start_send,
    start_recv,
):
    nv, girth, wall, stream = sizes
    half = girth // HALVES
    quads = wall_size // 4
    my_girth = lax.axis_index("girth")
    my_wall = lax.axis_index("wall")
    chip = my_wall // 2
    core = lax.rem(my_wall, 2)
    quad = my_wall // 4
    side = lax.rem(chip, 2)
    right = (lax.rem(my_girth + 1, girth_size), my_wall)
    left = (lax.rem(my_girth + girth_size - 1, girth_size), my_wall)
    partner = (my_girth, chip * 2 + 1 - core)

    def on_chip(other_chip):
        return (my_girth, other_chip * 2 + core)

    place = (core, 1 - core)
    is_lead = (side == 0, side == 1)
    is_first = (quad == 0, quad == quads - 1)
    is_last = (quad == quads - 1, quad == 0)
    mate = on_chip(quad * 2 + 1 - side)
    my_rows = pl.ds(pl.multiple_of(core * half, half), half)
    other_rows = pl.ds(pl.multiple_of((1 - core) * half, half), half)

    body_rows = pl.ds(HALO * wall, girth * wall)
    loads = [
        pltpu.make_async_copy(adj_hbm, adj.at[0, :, body_rows, :], load_sem.at[0]),
        pltpu.make_async_copy(low_hbm, low, load_sem.at[1]),
        pltpu.make_async_copy(rhs_hbm, rhs, load_sem.at[2]),
        pltpu.make_async_copy(gc_hbm, gc, load_sem.at[3]),
        pltpu.make_async_copy(sc_hbm, sc, load_sem.at[4]),
        pltpu.make_async_copy(piv_hbm, piv, load_sem.at[5]),
        pltpu.make_async_copy(upp_hbm, upp, load_sem.at[6]),
    ]
    for load in loads:
        load.start()

    barrier = pltpu.get_barrier_semaphore()

    def greet(device):
        pl.semaphore_signal(barrier, inc=1, device_id=device, device_id_type=MESH)

    greet(left)
    greet(right)
    greet(partner)
    greet(mate)

    @pl.when(quad > 0)
    def _():
        greet(on_chip(chip - 2))

        @pl.when(side == 0)
        def _():
            greet(on_chip(chip - 1))

    @pl.when(quad < quads - 1)
    def _():
        greet(on_chip(chip + 2))

        @pl.when(side == 1)
        def _():
            greet(on_chip(chip + 1))

    from_below = jnp.where(quad > 0, 2 - side, 0)
    from_above = jnp.where(quad < quads - 1, 1 + side, 0)

    def remote(src, dst, send_sem, recv_sem, device):
        return pltpu.make_async_remote_copy(
            src_ref=src,
            dst_ref=dst,
            send_sem=send_sem,
            recv_sem=recv_sem,
            device_id=device,
            device_id_type=MESH,
        )

    def halo_copies(sweep):
        field = adj.at[sweep]
        width = HALO * wall
        return [
            remote(
                field.at[:, pl.ds(width, width), :],
                field.at[:, pl.ds(width + girth * wall, width), :],
                halo_send.at[sweep, 0],
                halo_recv.at[sweep, 0],
                left,
            ),
            remote(
                field.at[:, pl.ds(girth * wall, width), :],
                field.at[:, pl.ds(0, width), :],
                halo_send.at[sweep, 1],
                halo_recv.at[sweep, 1],
                right,
            ),
        ]

    def coupling_column(d, w):
        return lambda j: couplings[d, :, j, w]

    def order(d, step):
        return step if d == 0 else wall - 1 - step

    def transpose_coupling(d, source):
        def one_row(i, carry):
            for j in range(nv):
                couplings[d, i, j] = jnp.swapaxes(source[i, j].astype(F32), 0, 1)
            return carry

        lax.fori_loop(0, nv, one_row, 0)

    def map_copy(d):
        return remote(
            other_map.at[d], half_map.at[d, place[d]], map_send.at[d], map_recv.at[d], partner
        )

    def make_map(d):
        for k in range(0, nv, 2):

            def advance(step, columns):
                column = coupling_column(d, order(d, step))
                return tuple(block_product(column, c) for c in columns)

            first = coupling_column(d, order(d, 0))
            columns = lax.fori_loop(1, wall, advance, (first(k), first(k + 1)))
            for shift in range(2):
                whole_column[...] = columns[shift]
                half_map[d, place[d], :, k + shift] = whole_column[:, my_rows, :]
                other_map[d, :, k + shift] = whole_column[:, other_rows, :]
        map_copy(d).start()

    def lead_map_copy(d):
        return remote(
            lead_map.at[d, 0], lead_map.at[d, 1], lead_map_send.at[d], lead_map_recv.at[d], mate
        )

    def make_lead_map(d):
        @pl.when(jnp.logical_and(is_lead[d], jnp.logical_not(is_first[d])))
        def _():
            def one_column(k, carry):
                lead_map[d, 0, :, k] = block_product(
                    lambda j: half_map[d, 1, :, j], half_map[d, 0, :, k]
                )
                return carry

            lax.fori_loop(0, nv, one_column, 0)
            lead_map_copy(d).start()

    lane = lax.broadcasted_iota(jnp.int32, (nv, wall, stream), 2)

    def make_source(sweep, g):
        def girth_layer(offset):
            rows = pl.ds(pl.multiple_of((g + HALO + offset) * wall, wall), wall)
            return adj[sweep, :, rows, :]

        here = girth_layer(0)
        beside_pair = girth_layer(-1) + girth_layer(1)
        distant_pair = girth_layer(-2) + girth_layer(2)
        before = jnp.where(lane == 0, 0.0, pltpu.roll(here, 1, 2))
        after = jnp.where(lane == stream - 1, 0.0, pltpu.roll(here, stream - 1, 2))
        neighbours = gc[:, g].astype(F32) * (beside_pair - 0.25 * distant_pair) + sc[
            :, g
        ].astype(F32) * (before + after)
        loaded = rhs[:, g] + neighbours
        staged[:, g] = block_product(
            lambda j: piv[:, j, g].astype(F32), loaded
        )

    def make_sources(sweep):
        def body(g, carry):
            make_source(sweep, g)
            return carry

        lax.fori_loop(HALO, girth - HALO, body, 0)
        for copy in halo_copies(sweep):
            copy.wait_recv()
        lax.fori_loop(0, HALO, body, 0)
        lax.fori_loop(girth - HALO, girth, body, 0)

        def one_variable(i, carry):
            work[i] = jnp.swapaxes(staged[i], 0, 1)
            return carry

        lax.fori_loop(0, nv, one_variable, 0)

    def advance_line(d, step, vector):
        w = order(d, step)
        return w, work[:, w] + block_product(coupling_column(d, w), vector)

    def find_tip(sweep, d):
        first = work[:, order(d, 0)]
        tip = lax.fori_loop(1, wall, lambda step, v: advance_line(d, step, v)[1], first)
        whole_column[...] = tip
        half_tip[sweep, d, place[d]] = whole_column[:, my_rows, :]
        other_tip[sweep, d] = whole_column[:, other_rows, :]
        tip_copy(sweep, d).start()

    def tip_copy(sweep, d):
        return remote(
            other_tip.at[sweep, d],
            half_tip.at[sweep, d, place[d]],
            tip_send.at[sweep, d],
            tip_recv.at[sweep, d],
            partner,
        )

    def lead_copy(sweep, d):
        return remote(
            lead_tip.at[sweep, d, 0],
            lead_tip.at[sweep, d, 1],
            lead_send.at[sweep, d],
            lead_recv.at[sweep, d],
            mate,
        )

    def pair_copy(sweep, d, target):
        sign = 1 if d == 0 else -1
        return remote(
            pair_out.at[sweep, d],
            entering.at[sweep, d],
            pair_send.at[sweep, d, target],
            pair_recv.at[sweep, d],
            on_chip(chip + sign * (target + 1)),
        )

    def start_copy(sweep, d):
        return remote(
            starts.at[sweep, d, 1 - place[d]],
            other_start.at[sweep, d],
            start_send.at[sweep, d],
            start_recv.at[sweep, d],
            partner,
        )

    def apply_half(d, which, vector):
        return block_product(lambda j: half_map[d, which, :, j], vector)

    def begin_chain(sweep, d):
        if sweep == 0:
            map_copy(d).wait_recv()
        tip_copy(sweep, d).wait_recv()

        @pl.when(is_lead[d])
        def _():
            lead_tip[sweep, d, 0] = half_tip[sweep, d, 1] + apply_half(
                d, 1, half_tip[sweep, d, 0]
            )
            lead_copy(sweep, d).start()

        if sweep == 0:
            make_lead_map(d)

    def finish_chain(sweep, d):
        first = is_first[d]
        later = jnp.logical_not(first)
        trail = jnp.logical_not(is_lead[d])

        @pl.when(trail)
        def _():
            lead_copy(sweep, d).wait_recv()

        if sweep == 0:

            @pl.when(jnp.logical_and(trail, later))
            def _():
                lead_map_copy(d).wait_recv()

        @pl.when(later)
        def _():
            pair_copy(sweep, d, 0).wait_recv()

        @pl.when(jnp.logical_and(is_lead[d], first))
        def _():
            starts[sweep, d, 0] = jnp.zeros_like(starts[sweep, d, 0])

        @pl.when(jnp.logical_and(is_lead[d], later))
        def _():
            starts[sweep, d, 0] = entering[sweep, d]

        @pl.when(jnp.logical_and(trail, first))
        def _():
            starts[sweep, d, 0] = lead_tip[sweep, d, 1]

        @pl.when(jnp.logical_and(trail, later))
        def _():
            starts[sweep, d, 0] = lead_tip[sweep, d, 1] + block_product(
                lambda j: lead_map[d, 1, :, j], entering[sweep, d]
            )

        middle = half_tip[sweep, d, 0] + apply_half(d, 0, starts[sweep, d, 0])
        starts[sweep, d, 1] = middle

        @pl.when(jnp.logical_and(trail, jnp.logical_not(is_last[d])))
        def _():
            pair_out[sweep, d] = half_tip[sweep, d, 1] + apply_half(d, 1, middle)
            pair_copy(sweep, d, 1).start()
            pair_copy(sweep, d, 0).start()

        start_copy(sweep, d).start()
        start_tip[:, my_rows, :] = starts[sweep, d, place[d]]
        start_copy(sweep, d).wait_recv()
        start_tip[:, other_rows, :] = other_start[sweep, d]

    def solve(d):
        def body(step, vector):
            w, vector = advance_line(d, step, vector)
            work[:, w] = vector
            return vector

        lax.fori_loop(0, wall, body, start_tip[...])

    def prepare_upper():
        loads[6].wait()
        transpose_coupling(1, upp)
        make_map(1)

    in_lower_half = quad < quads // 2

    loads[1].wait()
    transpose_coupling(0, low)
    pl.semaphore_wait(barrier, 4 + from_below + from_above)
    loads[0].wait()
    for copy in halo_copies(0):
        copy.start()
    make_map(0)
    for load in loads[2:6]:
        load.wait()

    for sweep in range(SWEEPS):
        make_sources(sweep)
        find_tip(sweep, 0)
        begin_chain(sweep, 0)
        if sweep == 0:
            pl.when(jnp.logical_not(in_lower_half))(prepare_upper)
        finish_chain(sweep, 0)
        solve(0)
        if sweep == 0:
            pl.when(in_lower_half)(prepare_upper)
        find_tip(sweep, 1)
        begin_chain(sweep, 1)
        finish_chain(sweep, 1)
        solve(1)
        last = sweep == SWEEPS - 1

        def one_variable(i, carry):
            values = jnp.swapaxes(work[i], 0, 1)
            if last:
                out_ref[i] = values
            else:
                adj[sweep + 1, i, body_rows] = values.reshape(girth * wall, stream)
            return carry

        lax.fori_loop(0, nv, one_variable, 0)
        if not last:
            for copy in halo_copies(sweep + 1):
                copy.start()

    for sweep in range(SWEEPS):
        for copy in halo_copies(sweep):
            copy.wait_send()
    for d in range(2):
        map_copy(d).wait_send()

        @pl.when(jnp.logical_and(is_lead[d], jnp.logical_not(is_first[d])))
        def _():
            lead_map_copy(d).wait_send()

        for sweep in range(SWEEPS):
            tip_copy(sweep, d).wait_send()
            start_copy(sweep, d).wait_send()

            @pl.when(is_lead[d])
            def _():
                lead_copy(sweep, d).wait_send()

            @pl.when(jnp.logical_and(jnp.logical_not(is_lead[d]), jnp.logical_not(is_last[d])))
            def _():
                pair_copy(sweep, d, 0).wait_send()
                pair_copy(sweep, d, 1).wait_send()


def on_device(
    girth_size,
    wall_size,
    adjoint_start,
    right_side,
    pivot_inverse,
    lower_coupling,
    upper_coupling,
    girth_coeff,
    stream_coeff,
):
    nv, girth, wall, stream = adjoint_start.shape
    half = girth // HALVES
    flat = (nv, girth * wall, stream)
    blocks = (nv, nv, girth, wall, stream)
    tip = (nv, half, stream)
    half_blocks = (nv, nv, half, stream)
    dma = pltpu.SemaphoreType.DMA
    out = pl.pallas_call(
        functools.partial(kernel, girth_size, wall_size, (nv, girth, wall, stream)),
        out_shape=jax.ShapeDtypeStruct((nv, girth, wall, stream), F32),
        in_specs=[pl.BlockSpec(memory_space=pl.ANY)] * 7,
        out_specs=pl.BlockSpec(memory_space=pltpu.VMEM),
        scratch_shapes=[
            pltpu.VMEM((SWEEPS, nv, (girth + 2 * HALO) * wall, stream), F32),
            pltpu.VMEM((nv, girth, wall, stream), F32),
            pltpu.VMEM(blocks, jnp.bfloat16),
            pltpu.VMEM(blocks, jnp.bfloat16),
            pltpu.VMEM(blocks, jnp.bfloat16),
            pltpu.VMEM((nv, girth, wall, stream), jnp.bfloat16),
            pltpu.VMEM((nv, girth, wall, stream), jnp.bfloat16),
            pltpu.VMEM((2, nv, nv, wall, girth, stream), F32),
            pltpu.VMEM((nv, wall, girth, stream), F32),
            pltpu.VMEM((nv, girth, wall, stream), F32),
            pltpu.VMEM((2, *half_blocks), F32),
            pltpu.VMEM((2, 2, *half_blocks), F32),
            pltpu.VMEM((2, 2, *half_blocks), F32),
            pltpu.VMEM((SWEEPS, 2, *tip), F32),
            pltpu.VMEM((SWEEPS, 2, 2, *tip), F32),
            pltpu.VMEM((SWEEPS, 2, 2, *tip), F32),
            pltpu.VMEM((SWEEPS, 2, *tip), F32),
            pltpu.VMEM((SWEEPS, 2, *tip), F32),
            pltpu.VMEM((SWEEPS, 2, 2, *tip), F32),
            pltpu.VMEM((SWEEPS, 2, *tip), F32),
            pltpu.VMEM((nv, girth, stream), F32),
            pltpu.VMEM((nv, girth, stream), F32),
            dma((7,)),
            dma((SWEEPS, 2)),
            dma((SWEEPS, 2)),
            dma((2,)),
            dma((2,)),
            dma((2,)),
            dma((2,)),
            dma((SWEEPS, 2)),
            dma((SWEEPS, 2)),
            dma((SWEEPS, 2)),
            dma((SWEEPS, 2)),
            dma((SWEEPS, 2, 2)),
            dma((SWEEPS, 2)),
            dma((SWEEPS, 2)),
            dma((SWEEPS, 2)),
        ],
        compiler_params=pltpu.CompilerParams(
            collective_id=0, has_side_effects=True, vmem_limit_bytes=62 * 2**20
        ),
    )(
        adjoint_start.reshape(flat),
        right_side,
        pivot_inverse,
        lower_coupling,
        upper_coupling,
        girth_coeff,
        stream_coeff,
    )
    return out


def solution(mesh):
    in_specs = (
        P(None, "girth", "wall", None),
        P(None, "girth", "wall", None),
        P(None, None, "girth", "wall", None),
        P(None, None, "girth", "wall", None),
        P(None, None, "girth", "wall", None),
        P(None, "girth", "wall", None),
        P(None, "girth", "wall", None),
    )
    out_specs = P(None, "girth", "wall", None)
    return jax.shard_map(
        functools.partial(on_device, mesh.shape["girth"], mesh.shape["wall"]),
        mesh=mesh,
        in_specs=in_specs,
        out_specs=out_specs,
        check_vma=False,
    )
```

```python
import functools

import jax
import jax.numpy as jnp
from jax import lax
from jax.experimental import pallas as pl
from jax.experimental.pallas import tpu as pltpu
from jax.sharding import PartitionSpec as P

SWEEPS = 2
HALO = 2
HALVES = 2
MESH = pl.DeviceIdType.MESH
F32 = jnp.float32


def block_product(column, vector):
    total = column(0) * vector[0][None]
    for j in range(1, vector.shape[0]):
        total = total + column(j) * vector[j][None]
    return total


def kernel(
    girth_size,
    wall_size,
    sizes,
    adj_hbm,
    rhs_hbm,
    piv_hbm,
    low_hbm,
    upp_hbm,
    gc_hbm,
    sc_hbm,
    out_ref,
    adj,
    rhs,
    piv,
    low,
    upp,
    gc,
    sc,
    couplings,
    work,
    staged,
    other_map,
    half_map,
    lead_map,
    products,
    other_cross,
    half_cross,
    chip_cross,
    trial,
    other_tip,
    half_tip,
    lead_tip,
    pair_out,
    entering,
    starts,
    other_start,
    start_tip,
    whole_column,
    mate_start,
    upper_answer,
    load_sem,
    halo_send,
    halo_recv,
    map_send,
    map_recv,
    lead_map_send,
    lead_map_recv,
    cross_send,
    cross_recv,
    chip_cross_send,
    chip_cross_recv,
    tip_send,
    tip_recv,
    lead_send,
    lead_recv,
    pair_send,
    pair_recv,
    start_send,
    start_recv,
):
    nv, girth, wall, stream = sizes
    half = girth // HALVES
    quads = wall_size // 4
    my_girth = lax.axis_index("girth")
    my_wall = lax.axis_index("wall")
    chip = my_wall // 2
    core = lax.rem(my_wall, 2)
    quad = my_wall // 4
    side = lax.rem(chip, 2)
    right = (lax.rem(my_girth + 1, girth_size), my_wall)
    left = (lax.rem(my_girth + girth_size - 1, girth_size), my_wall)
    partner = (my_girth, chip * 2 + 1 - core)

    def on_chip(other_chip):
        return (my_girth, other_chip * 2 + core)

    place = (core, 1 - core)
    is_lead = (side == 0, side == 1)
    is_first = (quad == 0, quad == quads - 1)
    is_last = (quad == quads - 1, quad == 0)
    mate = on_chip(quad * 2 + 1 - side)
    my_rows = pl.ds(pl.multiple_of(core * half, half), half)
    other_rows = pl.ds(pl.multiple_of((1 - core) * half, half), half)

    body_rows = pl.ds(HALO * wall, girth * wall)
    loads = [
        pltpu.make_async_copy(adj_hbm, adj.at[0, :, body_rows, :], load_sem.at[0]),
        pltpu.make_async_copy(low_hbm, low, load_sem.at[1]),
        pltpu.make_async_copy(rhs_hbm, rhs, load_sem.at[2]),
        pltpu.make_async_copy(gc_hbm, gc, load_sem.at[3]),
        pltpu.make_async_copy(sc_hbm, sc, load_sem.at[4]),
        pltpu.make_async_copy(piv_hbm, piv, load_sem.at[5]),
        pltpu.make_async_copy(upp_hbm, upp, load_sem.at[6]),
    ]
    for load in loads:
        load.start()

    barrier = pltpu.get_barrier_semaphore()

    def greet(device):
        pl.semaphore_signal(barrier, inc=1, device_id=device, device_id_type=MESH)

    greet(left)
    greet(right)
    greet(partner)
    greet(mate)

    @pl.when(quad > 0)
    def _():
        greet(on_chip(chip - 2))

        @pl.when(side == 0)
        def _():
            greet(on_chip(chip - 1))

    @pl.when(quad < quads - 1)
    def _():
        greet(on_chip(chip + 2))

        @pl.when(side == 1)
        def _():
            greet(on_chip(chip + 1))

    from_below = jnp.where(quad > 0, 2 - side, 0)
    from_above = jnp.where(quad < quads - 1, 1 + side, 0)

    def remote(src, dst, send_sem, recv_sem, device):
        return pltpu.make_async_remote_copy(
            src_ref=src,
            dst_ref=dst,
            send_sem=send_sem,
            recv_sem=recv_sem,
            device_id=device,
            device_id_type=MESH,
        )

    def halo_copies(sweep):
        field = adj.at[sweep]
        width = HALO * wall
        return [
            remote(
                field.at[:, pl.ds(width, width), :],
                field.at[:, pl.ds(width + girth * wall, width), :],
                halo_send.at[sweep, 0],
                halo_recv.at[sweep, 0],
                left,
            ),
            remote(
                field.at[:, pl.ds(girth * wall, width), :],
                field.at[:, pl.ds(0, width), :],
                halo_send.at[sweep, 1],
                halo_recv.at[sweep, 1],
                right,
            ),
        ]

    def coupling_column(d, w):
        return lambda j: couplings[d, :, j, w]

    def order(d, step):
        return step if d == 0 else wall - 1 - step

    def transpose_coupling(d, source):
        def one_row(i, carry):
            for j in range(nv):
                couplings[d, i, j] = jnp.swapaxes(source[i, j].astype(F32), 0, 1)
            return carry

        lax.fori_loop(0, nv, one_row, 0)

    def map_copy(d):
        return remote(
            other_map.at[d], half_map.at[d, place[d]], map_send.at[d], map_recv.at[d], partner
        )

    def keep_halves(column, half_ref, other_ref, k):
        whole_column[...] = column
        half_ref[:, k] = whole_column[:, my_rows, :]
        other_ref[:, k] = whole_column[:, other_rows, :]

    def make_lower_map():
        first = coupling_column(0, 0)
        for k in range(0, nv, 2):

            def advance(w, columns):
                column = coupling_column(0, w)
                columns = tuple(block_product(column, c) for c in columns)
                products[:, k, w] = columns[0]
                products[:, k + 1, w] = columns[1]
                return columns

            products[:, k, 0] = first(k)
            products[:, k + 1, 0] = first(k + 1)
            columns = lax.fori_loop(1, wall, advance, (first(k), first(k + 1)))
            for shift in range(2):
                keep_halves(
                    columns[shift], half_map.at[0, place[0]], other_map.at[0], k + shift
                )
        map_copy(0).start()

    def cross_copy():
        return remote(
            other_cross, half_cross.at[core], cross_send, cross_recv, partner
        )

    def chip_cross_copy():
        return remote(
            chip_cross.at[0], chip_cross.at[1], chip_cross_send, chip_cross_recv, mate
        )

    def make_upper_maps():
        first = coupling_column(1, wall - 1)
        for k in range(nv):

            def advance(step, columns):
                w = order(1, step)
                column = coupling_column(1, w)
                return (
                    block_product(column, columns[0]),
                    products[:, k, w] + block_product(column, columns[1]),
                )

            columns = lax.fori_loop(1, wall, advance, (first(k), products[:, k, wall - 1]))
            keep_halves(columns[0], half_map.at[1, place[1]], other_map.at[1], k)
            keep_halves(columns[1], half_cross.at[core], other_cross, k)
        map_copy(1).start()
        cross_copy().start()

    def make_chip_cross():
        @pl.when(is_lead[1])
        def _():
            def one_column(k, carry):
                column = block_product(lambda j: half_cross[1, :, j], half_map[0, 0, :, k])
                column = apply_half(1, 1, column)
                chip_cross[0, :, k] = half_cross[0, :, k] + column
                return carry

            lax.fori_loop(0, nv, one_column, 0)
            chip_cross_copy().start()

    def lead_map_copy(d):
        return remote(
            lead_map.at[d, 0], lead_map.at[d, 1], lead_map_send.at[d], lead_map_recv.at[d], mate
        )

    def make_lead_map(d):
        @pl.when(jnp.logical_and(is_lead[d], jnp.logical_not(is_first[d])))
        def _():
            def one_column(k, carry):
                lead_map[d, 0, :, k] = block_product(
                    lambda j: half_map[d, 1, :, j], half_map[d, 0, :, k]
                )
                return carry

            lax.fori_loop(0, nv, one_column, 0)
            lead_map_copy(d).start()

    lane = lax.broadcasted_iota(jnp.int32, (nv, wall, stream), 2)

    def make_source(sweep, g):
        def girth_layer(offset):
            rows = pl.ds(pl.multiple_of((g + HALO + offset) * wall, wall), wall)
            return adj[sweep, :, rows, :]

        here = girth_layer(0)
        beside_pair = girth_layer(-1) + girth_layer(1)
        distant_pair = girth_layer(-2) + girth_layer(2)
        before = jnp.where(lane == 0, 0.0, pltpu.roll(here, 1, 2))
        after = jnp.where(lane == stream - 1, 0.0, pltpu.roll(here, stream - 1, 2))
        neighbours = gc[:, g].astype(F32) * (beside_pair - 0.25 * distant_pair) + sc[
            :, g
        ].astype(F32) * (before + after)
        loaded = rhs[:, g] + neighbours
        staged[:, g] = block_product(
            lambda j: piv[:, j, g].astype(F32), loaded
        )

    def make_sources(sweep):
        def body(g, carry):
            make_source(sweep, g)
            return carry

        lax.fori_loop(HALO, girth - HALO, body, 0)
        for copy in halo_copies(sweep):
            copy.wait_recv()
        lax.fori_loop(0, HALO, body, 0)
        lax.fori_loop(girth - HALO, girth, body, 0)

        def one_variable(i, carry):
            work[i] = jnp.swapaxes(staged[i], 0, 1)
            return carry

        lax.fori_loop(0, nv, one_variable, 0)

    def advance_line(d, step, vector):
        w = order(d, step)
        return w, work[:, w] + block_product(coupling_column(d, w), vector)

    def send_tip(sweep, d, tip):
        whole_column[...] = tip
        half_tip[sweep, d, place[d]] = whole_column[:, my_rows, :]
        other_tip[sweep, d] = whole_column[:, other_rows, :]
        tip_copy(sweep, d).start()

    def find_lower_tip(sweep):
        def body(w, vector):
            vector = advance_line(0, w, vector)[1]
            trial[:, w] = vector
            return vector

        trial[:, 0] = work[:, 0]
        send_tip(sweep, 0, lax.fori_loop(1, wall, body, work[:, 0]))

    def find_upper_tip(sweep):
        def body(step, vector):
            w = order(1, step)
            return trial[:, w] + block_product(coupling_column(1, w), vector)

        send_tip(sweep, 1, lax.fori_loop(1, wall, body, trial[:, wall - 1]))

    def tip_copy(sweep, d):
        return remote(
            other_tip.at[sweep, d],
            half_tip.at[sweep, d, place[d]],
            tip_send.at[sweep, d],
            tip_recv.at[sweep, d],
            partner,
        )

    def lead_copy(sweep, d):
        return remote(
            lead_tip.at[sweep, d, 0],
            lead_tip.at[sweep, d, 1],
            lead_send.at[sweep, d],
            lead_recv.at[sweep, d],
            mate,
        )

    def pair_copy(sweep, d, target):
        sign = 1 if d == 0 else -1
        return remote(
            pair_out.at[sweep, d],
            entering.at[sweep, d],
            pair_send.at[sweep, d, target],
            pair_recv.at[sweep, d],
            on_chip(chip + sign * (target + 1)),
        )

    def start_copy(sweep, d):
        return remote(
            starts.at[sweep, d, 1 - place[d]],
            other_start.at[sweep, d],
            start_send.at[sweep, d],
            start_recv.at[sweep, d],
            partner,
        )

    def apply_half(d, which, vector):
        return block_product(lambda j: half_map[d, which, :, j], vector)

    def apply_cross(which, vector):
        return block_product(lambda j: half_cross[which, :, j], vector)

    def begin_lower(sweep):
        if sweep == 0:
            map_copy(0).wait_recv()
        tip_copy(sweep, 0).wait_recv()

        @pl.when(is_lead[0])
        def _():
            lead_tip[sweep, 0, 0] = half_tip[sweep, 0, 1] + apply_half(
                0, 1, half_tip[sweep, 0, 0]
            )
            lead_copy(sweep, 0).start()

        if sweep == 0:
            make_lead_map(0)

    def begin_upper(sweep):
        if sweep == 0:
            map_copy(1).wait_recv()
            cross_copy().wait_recv()
        tip_copy(sweep, 1).wait_recv()

        @pl.when(is_lead[1])
        def _():
            reached = half_tip[sweep, 1, 0] + apply_cross(1, half_tip[sweep, 0, 0])
            lead_tip[sweep, 1, 0] = half_tip[sweep, 1, 1] + apply_half(1, 1, reached)
            lead_copy(sweep, 1).start()

        if sweep == 0:
            make_chip_cross()
            make_lead_map(1)

    def take_entering(sweep, d):
        @pl.when(is_first[d])
        def _():
            entering[sweep, d] = jnp.zeros_like(entering[sweep, d])

        @pl.when(jnp.logical_not(is_first[d]))
        def _():
            pair_copy(sweep, d, 0).wait_recv()

    def apply_lead_map(d, which, vector):
        return block_product(lambda j: lead_map[d, which, :, j], vector)

    def finish_lower(sweep):
        later = jnp.logical_not(is_first[0])
        trail = jnp.logical_not(is_lead[0])

        @pl.when(trail)
        def _():
            lead_copy(sweep, 0).wait_recv()

        if sweep == 0:

            @pl.when(jnp.logical_and(trail, later))
            def _():
                lead_map_copy(0).wait_recv()

        take_entering(sweep, 0)

        @pl.when(is_lead[0])
        def _():
            starts[sweep, 0, 0] = entering[sweep, 0]

        @pl.when(jnp.logical_and(trail, is_first[0]))
        def _():
            starts[sweep, 0, 0] = lead_tip[sweep, 0, 1]

        @pl.when(jnp.logical_and(trail, later))
        def _():
            starts[sweep, 0, 0] = lead_tip[sweep, 0, 1] + apply_lead_map(
                0, 1, entering[sweep, 0]
            )

        middle = half_tip[sweep, 0, 0] + apply_half(0, 0, starts[sweep, 0, 0])
        starts[sweep, 0, 1] = middle

        @pl.when(jnp.logical_and(trail, jnp.logical_not(is_last[0])))
        def _():
            pair_out[sweep, 0] = half_tip[sweep, 0, 1] + apply_half(0, 1, middle)
            pair_copy(sweep, 0, 1).start()
            pair_copy(sweep, 0, 0).start()

        start_copy(sweep, 0).start()

    def finish_upper(sweep):
        later = jnp.logical_not(is_first[1])
        trail = jnp.logical_not(is_lead[1])

        @pl.when(trail)
        def _():
            lead_copy(sweep, 1).wait_recv()
            if sweep == 0:
                chip_cross_copy().wait_recv()
            mate_start[...] = lead_tip[sweep, 0, 0]

        @pl.when(jnp.logical_and(trail, jnp.logical_not(is_first[0])))
        def _():
            mate_start[...] = mate_start[...] + apply_lead_map(0, 0, entering[sweep, 0])

        @pl.when(trail)
        def _():
            starts[sweep, 1, 0] = lead_tip[sweep, 1, 1] + block_product(
                lambda j: chip_cross[1, :, j], mate_start[...]
            )

        lower_answer = half_tip[sweep, 1, 0] + apply_cross(1, starts[sweep, 0, 1])
        upper_answer[...] = half_tip[sweep, 1, 1] + apply_cross(0, starts[sweep, 0, 0])

        if sweep == 0:

            @pl.when(jnp.logical_and(trail, later))
            def _():
                lead_map_copy(1).wait_recv()

        take_entering(sweep, 1)

        @pl.when(is_lead[1])
        def _():
            starts[sweep, 1, 0] = entering[sweep, 1]

        @pl.when(jnp.logical_and(trail, later))
        def _():
            starts[sweep, 1, 0] = starts[sweep, 1, 0] + apply_lead_map(
                1, 1, entering[sweep, 1]
            )

        middle = lower_answer + apply_half(1, 0, starts[sweep, 1, 0])
        starts[sweep, 1, 1] = middle

        @pl.when(jnp.logical_and(trail, jnp.logical_not(is_last[1])))
        def _():
            pair_out[sweep, 1] = upper_answer[...] + apply_half(1, 1, middle)
            pair_copy(sweep, 1, 1).start()
            pair_copy(sweep, 1, 0).start()

        start_copy(sweep, 1).start()

    def solve_from_start(sweep, d):
        start_tip[:, my_rows, :] = starts[sweep, d, place[d]]
        start_copy(sweep, d).wait_recv()
        start_tip[:, other_rows, :] = other_start[sweep, d]
        solve(d)

    def solve(d):
        def body(step, vector):
            w, vector = advance_line(d, step, vector)
            work[:, w] = vector
            return vector

        lax.fori_loop(0, wall, body, start_tip[...])

    def prepare_upper():
        loads[6].wait()
        transpose_coupling(1, upp)
        make_upper_maps()
        find_upper_tip(0)
        begin_upper(0)

    in_lower_half = quad < quads // 2

    loads[1].wait()
    transpose_coupling(0, low)
    pl.semaphore_wait(barrier, 4 + from_below + from_above)
    loads[0].wait()
    for copy in halo_copies(0):
        copy.start()
    make_lower_map()
    for load in loads[2:6]:
        load.wait()

    for sweep in range(SWEEPS):
        make_sources(sweep)
        find_lower_tip(sweep)
        if sweep > 0:
            find_upper_tip(sweep)
        begin_lower(sweep)
        if sweep == 0:
            pl.when(jnp.logical_not(in_lower_half))(prepare_upper)
        else:
            begin_upper(sweep)
        finish_lower(sweep)
        if sweep == 0:
            pl.when(in_lower_half)(prepare_upper)

        @pl.when(jnp.logical_not(is_first[1]))
        def _():
            solve_from_start(sweep, 0)

        finish_upper(sweep)

        @pl.when(is_first[1])
        def _():
            solve_from_start(sweep, 0)

        solve_from_start(sweep, 1)
        last = sweep == SWEEPS - 1

        def one_variable(i, carry):
            values = jnp.swapaxes(work[i], 0, 1)
            if last:
                out_ref[i] = values
            else:
                adj[sweep + 1, i, body_rows] = values.reshape(girth * wall, stream)
            return carry

        lax.fori_loop(0, nv, one_variable, 0)
        if not last:
            for copy in halo_copies(sweep + 1):
                copy.start()

    for sweep in range(SWEEPS):
        for copy in halo_copies(sweep):
            copy.wait_send()
    cross_copy().wait_send()

    @pl.when(is_lead[1])
    def _():
        chip_cross_copy().wait_send()

    for d in range(2):
        map_copy(d).wait_send()

        @pl.when(jnp.logical_and(is_lead[d], jnp.logical_not(is_first[d])))
        def _():
            lead_map_copy(d).wait_send()

        for sweep in range(SWEEPS):
            tip_copy(sweep, d).wait_send()
            start_copy(sweep, d).wait_send()

            @pl.when(is_lead[d])
            def _():
                lead_copy(sweep, d).wait_send()

            @pl.when(jnp.logical_and(jnp.logical_not(is_lead[d]), jnp.logical_not(is_last[d])))
            def _():
                pair_copy(sweep, d, 0).wait_send()
                pair_copy(sweep, d, 1).wait_send()


def on_device(
    girth_size,
    wall_size,
    adjoint_start,
    right_side,
    pivot_inverse,
    lower_coupling,
    upper_coupling,
    girth_coeff,
    stream_coeff,
):
    nv, girth, wall, stream = adjoint_start.shape
    half = girth // HALVES
    flat = (nv, girth * wall, stream)
    blocks = (nv, nv, girth, wall, stream)
    tip = (nv, half, stream)
    half_blocks = (nv, nv, half, stream)
    dma = pltpu.SemaphoreType.DMA
    out = pl.pallas_call(
        functools.partial(kernel, girth_size, wall_size, (nv, girth, wall, stream)),
        out_shape=jax.ShapeDtypeStruct((nv, girth, wall, stream), F32),
        in_specs=[pl.BlockSpec(memory_space=pl.ANY)] * 7,
        out_specs=pl.BlockSpec(memory_space=pltpu.VMEM),
        scratch_shapes=[
            pltpu.VMEM((SWEEPS, nv, (girth + 2 * HALO) * wall, stream), F32),
            pltpu.VMEM((nv, girth, wall, stream), F32),
            pltpu.VMEM(blocks, jnp.bfloat16),
            pltpu.VMEM(blocks, jnp.bfloat16),
            pltpu.VMEM(blocks, jnp.bfloat16),
            pltpu.VMEM((nv, girth, wall, stream), jnp.bfloat16),
            pltpu.VMEM((nv, girth, wall, stream), jnp.bfloat16),
            pltpu.VMEM((2, nv, nv, wall, girth, stream), F32),
            pltpu.VMEM((nv, wall, girth, stream), F32),
            pltpu.VMEM((nv, girth, wall, stream), F32),
            pltpu.VMEM((2, *half_blocks), F32),
            pltpu.VMEM((2, 2, *half_blocks), F32),
            pltpu.VMEM((2, 2, *half_blocks), F32),
            pltpu.VMEM((nv, nv, wall, girth, stream), F32),
            pltpu.VMEM(half_blocks, F32),
            pltpu.VMEM((2, *half_blocks), F32),
            pltpu.VMEM((2, *half_blocks), F32),
            pltpu.VMEM((nv, wall, girth, stream), F32),
            pltpu.VMEM((SWEEPS, 2, *tip), F32),
            pltpu.VMEM((SWEEPS, 2, 2, *tip), F32),
            pltpu.VMEM((SWEEPS, 2, 2, *tip), F32),
            pltpu.VMEM((SWEEPS, 2, *tip), F32),
            pltpu.VMEM((SWEEPS, 2, *tip), F32),
            pltpu.VMEM((SWEEPS, 2, 2, *tip), F32),
            pltpu.VMEM((SWEEPS, 2, *tip), F32),
            pltpu.VMEM((nv, girth, stream), F32),
            pltpu.VMEM((nv, girth, stream), F32),
            pltpu.VMEM(tip, F32),
            pltpu.VMEM(tip, F32),
            dma((7,)),
            dma((SWEEPS, 2)),
            dma((SWEEPS, 2)),
            dma((2,)),
            dma((2,)),
            dma((2,)),
            dma((2,)),
            dma,
            dma,
            dma,
            dma,
            dma((SWEEPS, 2)),
            dma((SWEEPS, 2)),
            dma((SWEEPS, 2)),
            dma((SWEEPS, 2)),
            dma((SWEEPS, 2, 2)),
            dma((SWEEPS, 2)),
            dma((SWEEPS, 2)),
            dma((SWEEPS, 2)),
        ],
        compiler_params=pltpu.CompilerParams(
            collective_id=0, has_side_effects=True, vmem_limit_bytes=62 * 2**20
        ),
    )(
        adjoint_start.reshape(flat),
        right_side,
        pivot_inverse,
        lower_coupling,
        upper_coupling,
        girth_coeff,
        stream_coeff,
    )
    return out


def solution(mesh):
    in_specs = (
        P(None, "girth", "wall", None),
        P(None, "girth", "wall", None),
        P(None, None, "girth", "wall", None),
        P(None, None, "girth", "wall", None),
        P(None, None, "girth", "wall", None),
        P(None, "girth", "wall", None),
        P(None, "girth", "wall", None),
    )
    out_specs = P(None, "girth", "wall", None)
    return jax.shard_map(
        functools.partial(on_device, mesh.shape["girth"], mesh.shape["wall"]),
        mesh=mesh,
        in_specs=in_specs,
        out_specs=out_specs,
        check_vma=False,
    )
```

```python
import functools

import jax
import jax.numpy as jnp
from jax import lax
from jax.experimental import pallas as pl
from jax.experimental.pallas import tpu as pltpu
from jax.sharding import PartitionSpec as P

SWEEPS = 2
HALO = 2
HALVES = 2
MESH = pl.DeviceIdType.MESH
F32 = jnp.float32


def block_product(column, vector):
    terms = [column(j) * vector[j][None] for j in range(vector.shape[0])]
    while len(terms) > 1:
        pairs = [a + b for a, b in zip(terms[::2], terms[1::2])]
        terms = pairs + terms[len(pairs) * 2 :]
    return terms[0]


def kernel(
    girth_size,
    wall_size,
    sizes,
    adj_hbm,
    rhs_hbm,
    piv_hbm,
    low_hbm,
    upp_hbm,
    gc_hbm,
    sc_hbm,
    out_ref,
    adj,
    rhs,
    piv,
    low,
    upp,
    gc,
    sc,
    couplings,
    work,
    staged,
    other_map,
    half_map,
    lead_map,
    products,
    other_cross,
    half_cross,
    chip_cross,
    trial,
    other_tip,
    half_tip,
    lead_tip,
    pair_out,
    entering,
    starts,
    other_start,
    start_tip,
    whole_column,
    mate_start,
    upper_answer,
    load_sem,
    halo_send,
    halo_recv,
    map_send,
    map_recv,
    lead_map_send,
    lead_map_recv,
    cross_send,
    cross_recv,
    chip_cross_send,
    chip_cross_recv,
    tip_send,
    tip_recv,
    lead_send,
    lead_recv,
    pair_send,
    pair_recv,
    start_send,
    start_recv,
):
    nv, girth, wall, stream = sizes
    half = girth // HALVES
    quads = wall_size // 4
    my_girth = lax.axis_index("girth")
    my_wall = lax.axis_index("wall")
    chip = my_wall // 2
    core = lax.rem(my_wall, 2)
    quad = my_wall // 4
    side = lax.rem(chip, 2)
    right = (lax.rem(my_girth + 1, girth_size), my_wall)
    left = (lax.rem(my_girth + girth_size - 1, girth_size), my_wall)
    partner = (my_girth, chip * 2 + 1 - core)

    def on_chip(other_chip):
        return (my_girth, other_chip * 2 + core)

    place = (core, 1 - core)
    is_lead = (side == 0, side == 1)
    is_first = (quad == 0, quad == quads - 1)
    is_last = (quad == quads - 1, quad == 0)
    mate = on_chip(quad * 2 + 1 - side)
    my_rows = pl.ds(pl.multiple_of(core * half, half), half)
    other_rows = pl.ds(pl.multiple_of((1 - core) * half, half), half)

    body_rows = pl.ds(HALO * wall, girth * wall)
    loads = [
        pltpu.make_async_copy(adj_hbm, adj.at[0, :, body_rows, :], load_sem.at[0]),
        pltpu.make_async_copy(low_hbm, low, load_sem.at[1]),
        pltpu.make_async_copy(rhs_hbm, rhs, load_sem.at[2]),
        pltpu.make_async_copy(gc_hbm, gc, load_sem.at[3]),
        pltpu.make_async_copy(sc_hbm, sc, load_sem.at[4]),
        pltpu.make_async_copy(piv_hbm, piv, load_sem.at[5]),
        pltpu.make_async_copy(upp_hbm, upp, load_sem.at[6]),
    ]
    for load in loads:
        load.start()

    barrier = pltpu.get_barrier_semaphore()

    def greet(device):
        pl.semaphore_signal(barrier, inc=1, device_id=device, device_id_type=MESH)

    greet(left)
    greet(right)
    greet(partner)
    greet(mate)

    @pl.when(quad > 0)
    def _():
        greet(on_chip(chip - 2))

        @pl.when(side == 0)
        def _():
            greet(on_chip(chip - 1))

    @pl.when(quad < quads - 1)
    def _():
        greet(on_chip(chip + 2))

        @pl.when(side == 1)
        def _():
            greet(on_chip(chip + 1))

    from_below = jnp.where(quad > 0, 2 - side, 0)
    from_above = jnp.where(quad < quads - 1, 1 + side, 0)

    def remote(src, dst, send_sem, recv_sem, device):
        return pltpu.make_async_remote_copy(
            src_ref=src,
            dst_ref=dst,
            send_sem=send_sem,
            recv_sem=recv_sem,
            device_id=device,
            device_id_type=MESH,
        )

    def halo_copies(sweep):
        field = adj.at[sweep]
        width = HALO * wall
        return [
            remote(
                field.at[:, pl.ds(width, width), :],
                field.at[:, pl.ds(width + girth * wall, width), :],
                halo_send.at[sweep, 0],
                halo_recv.at[sweep, 0],
                left,
            ),
            remote(
                field.at[:, pl.ds(girth * wall, width), :],
                field.at[:, pl.ds(0, width), :],
                halo_send.at[sweep, 1],
                halo_recv.at[sweep, 1],
                right,
            ),
        ]

    def coupling_column(d, w):
        return lambda j: couplings[d, :, j, w]

    def line_loop(begin, body, carry):
        return lax.fori_loop(begin, wall, body, carry, unroll=5 if begin else 4)

    def order(d, step):
        return step if d == 0 else wall - 1 - step

    def transpose_coupling(d, source):
        def one_row(i, carry):
            for j in range(nv):
                couplings[d, i, j] = jnp.swapaxes(source[i, j].astype(F32), 0, 1)
            return carry

        lax.fori_loop(0, nv, one_row, 0)

    def map_copy(d):
        return remote(
            other_map.at[d], half_map.at[d, place[d]], map_send.at[d], map_recv.at[d], partner
        )

    def keep_halves(column, half_ref, other_ref, k):
        whole_column[...] = column
        half_ref[:, k] = whole_column[:, my_rows, :]
        other_ref[:, k] = whole_column[:, other_rows, :]

    def make_lower_map():
        first = coupling_column(0, 0)
        for k in range(0, nv, 2):

            def advance(w, columns):
                column = coupling_column(0, w)
                columns = tuple(block_product(column, c) for c in columns)
                products[:, k, w] = columns[0]
                products[:, k + 1, w] = columns[1]
                return columns

            products[:, k, 0] = first(k)
            products[:, k + 1, 0] = first(k + 1)
            columns = line_loop(1, advance, (first(k), first(k + 1)))
            for shift in range(2):
                keep_halves(
                    columns[shift], half_map.at[0, place[0]], other_map.at[0], k + shift
                )
        map_copy(0).start()

    def cross_copy():
        return remote(
            other_cross, half_cross.at[core], cross_send, cross_recv, partner
        )

    def chip_cross_copy():
        return remote(
            chip_cross.at[0], chip_cross.at[1], chip_cross_send, chip_cross_recv, mate
        )

    def make_upper_maps():
        first = coupling_column(1, wall - 1)
        for k in range(nv):

            def advance(step, columns):
                w = order(1, step)
                column = coupling_column(1, w)
                return (
                    block_product(column, columns[0]),
                    products[:, k, w] + block_product(column, columns[1]),
                )

            columns = line_loop(1, advance, (first(k), products[:, k, wall - 1]))
            keep_halves(columns[0], half_map.at[1, place[1]], other_map.at[1], k)
            keep_halves(columns[1], half_cross.at[core], other_cross, k)
        map_copy(1).start()
        cross_copy().start()

    def make_chip_cross():
        @pl.when(is_lead[1])
        def _():
            def one_column(k, carry):
                column = block_product(lambda j: half_cross[1, :, j], half_map[0, 0, :, k])
                column = apply_half(1, 1, column)
                chip_cross[0, :, k] = half_cross[0, :, k] + column
                return carry

            lax.fori_loop(0, nv, one_column, 0)
            chip_cross_copy().start()

    def lead_map_copy(d):
        return remote(
            lead_map.at[d, 0], lead_map.at[d, 1], lead_map_send.at[d], lead_map_recv.at[d], mate
        )

    def make_lead_map(d):
        @pl.when(jnp.logical_and(is_lead[d], jnp.logical_not(is_first[d])))
        def _():
            def one_column(k, carry):
                lead_map[d, 0, :, k] = block_product(
                    lambda j: half_map[d, 1, :, j], half_map[d, 0, :, k]
                )
                return carry

            lax.fori_loop(0, nv, one_column, 0)
            lead_map_copy(d).start()

    lane = lax.broadcasted_iota(jnp.int32, (nv, wall, stream), 2)

    def make_source(sweep, g):
        def girth_layer(offset):
            rows = pl.ds(pl.multiple_of((g + HALO + offset) * wall, wall), wall)
            return adj[sweep, :, rows, :]

        here = girth_layer(0)
        beside_pair = girth_layer(-1) + girth_layer(1)
        distant_pair = girth_layer(-2) + girth_layer(2)
        before = jnp.where(lane == 0, 0.0, pltpu.roll(here, 1, 2))
        after = jnp.where(lane == stream - 1, 0.0, pltpu.roll(here, stream - 1, 2))
        neighbours = gc[:, g].astype(F32) * (beside_pair - 0.25 * distant_pair) + sc[
            :, g
        ].astype(F32) * (before + after)
        loaded = rhs[:, g] + neighbours
        staged[:, g] = block_product(
            lambda j: piv[:, j, g].astype(F32), loaded
        )

    def make_sources(sweep):
        def body(g, carry):
            make_source(sweep, g)
            return carry

        lax.fori_loop(HALO, girth - HALO, body, 0)
        for copy in halo_copies(sweep):
            copy.wait_recv()
        lax.fori_loop(0, HALO, body, 0)
        lax.fori_loop(girth - HALO, girth, body, 0)

        def one_variable(i, carry):
            work[i] = jnp.swapaxes(staged[i], 0, 1)
            return carry

        lax.fori_loop(0, nv, one_variable, 0)

    def advance_line(d, step, vector):
        w = order(d, step)
        return w, work[:, w] + block_product(coupling_column(d, w), vector)

    def send_tip(sweep, d, tip):
        whole_column[...] = tip
        half_tip[sweep, d, place[d]] = whole_column[:, my_rows, :]
        other_tip[sweep, d] = whole_column[:, other_rows, :]
        tip_copy(sweep, d).start()

    def find_lower_tip(sweep):
        def body(w, vector):
            vector = advance_line(0, w, vector)[1]
            trial[:, w] = vector
            return vector

        trial[:, 0] = work[:, 0]
        send_tip(sweep, 0, line_loop(1, body, work[:, 0]))

    def find_upper_tip(sweep):
        def body(step, vector):
            w = order(1, step)
            return trial[:, w] + block_product(coupling_column(1, w), vector)

        send_tip(sweep, 1, line_loop(1, body, trial[:, wall - 1]))

    def tip_copy(sweep, d):
        return remote(
            other_tip.at[sweep, d],
            half_tip.at[sweep, d, place[d]],
            tip_send.at[sweep, d],
            tip_recv.at[sweep, d],
            partner,
        )

    def lead_copy(sweep, d):
        return remote(
            lead_tip.at[sweep, d, 0],
            lead_tip.at[sweep, d, 1],
            lead_send.at[sweep, d],
            lead_recv.at[sweep, d],
            mate,
        )

    def pair_copy(sweep, d, target):
        sign = 1 if d == 0 else -1
        return remote(
            pair_out.at[sweep, d],
            entering.at[sweep, d],
            pair_send.at[sweep, d, target],
            pair_recv.at[sweep, d],
            on_chip(chip + sign * (target + 1)),
        )

    def start_copy(sweep, d):
        return remote(
            starts.at[sweep, d, 1 - place[d]],
            other_start.at[sweep, d],
            start_send.at[sweep, d],
            start_recv.at[sweep, d],
            partner,
        )

    def apply_half(d, which, vector):
        return block_product(lambda j: half_map[d, which, :, j], vector)

    def apply_cross(which, vector):
        return block_product(lambda j: half_cross[which, :, j], vector)

    def begin_lower(sweep):
        if sweep == 0:
            map_copy(0).wait_recv()
        tip_copy(sweep, 0).wait_recv()

        @pl.when(is_lead[0])
        def _():
            lead_tip[sweep, 0, 0] = half_tip[sweep, 0, 1] + apply_half(
                0, 1, half_tip[sweep, 0, 0]
            )
            lead_copy(sweep, 0).start()

        if sweep == 0:
            make_lead_map(0)

    def begin_upper(sweep):
        if sweep == 0:
            map_copy(1).wait_recv()
            cross_copy().wait_recv()
        tip_copy(sweep, 1).wait_recv()

        @pl.when(is_lead[1])
        def _():
            reached = half_tip[sweep, 1, 0] + apply_cross(1, half_tip[sweep, 0, 0])
            lead_tip[sweep, 1, 0] = half_tip[sweep, 1, 1] + apply_half(1, 1, reached)
            lead_copy(sweep, 1).start()

        if sweep == 0:
            make_chip_cross()
            make_lead_map(1)

    def take_entering(sweep, d):
        @pl.when(is_first[d])
        def _():
            entering[sweep, d] = jnp.zeros_like(entering[sweep, d])

        @pl.when(jnp.logical_not(is_first[d]))
        def _():
            pair_copy(sweep, d, 0).wait_recv()

    def apply_lead_map(d, which, vector):
        return block_product(lambda j: lead_map[d, which, :, j], vector)

    def finish_lower(sweep):
        later = jnp.logical_not(is_first[0])
        trail = jnp.logical_not(is_lead[0])

        @pl.when(trail)
        def _():
            lead_copy(sweep, 0).wait_recv()

        if sweep == 0:

            @pl.when(jnp.logical_and(trail, later))
            def _():
                lead_map_copy(0).wait_recv()

        take_entering(sweep, 0)

        @pl.when(is_lead[0])
        def _():
            starts[sweep, 0, 0] = entering[sweep, 0]

        @pl.when(jnp.logical_and(trail, is_first[0]))
        def _():
            starts[sweep, 0, 0] = lead_tip[sweep, 0, 1]

        @pl.when(jnp.logical_and(trail, later))
        def _():
            starts[sweep, 0, 0] = lead_tip[sweep, 0, 1] + apply_lead_map(
                0, 1, entering[sweep, 0]
            )

        middle = half_tip[sweep, 0, 0] + apply_half(0, 0, starts[sweep, 0, 0])
        starts[sweep, 0, 1] = middle

        @pl.when(jnp.logical_and(trail, jnp.logical_not(is_last[0])))
        def _():
            pair_out[sweep, 0] = half_tip[sweep, 0, 1] + apply_half(0, 1, middle)
            pair_copy(sweep, 0, 1).start()
            pair_copy(sweep, 0, 0).start()

        start_copy(sweep, 0).start()

    def finish_upper(sweep):
        later = jnp.logical_not(is_first[1])
        trail = jnp.logical_not(is_lead[1])

        @pl.when(trail)
        def _():
            lead_copy(sweep, 1).wait_recv()
            if sweep == 0:
                chip_cross_copy().wait_recv()
            mate_start[...] = lead_tip[sweep, 0, 0]

        @pl.when(jnp.logical_and(trail, jnp.logical_not(is_first[0])))
        def _():
            mate_start[...] = mate_start[...] + apply_lead_map(0, 0, entering[sweep, 0])

        @pl.when(trail)
        def _():
            starts[sweep, 1, 0] = lead_tip[sweep, 1, 1] + block_product(
                lambda j: chip_cross[1, :, j], mate_start[...]
            )

        lower_answer = half_tip[sweep, 1, 0] + apply_cross(1, starts[sweep, 0, 1])
        upper_answer[...] = half_tip[sweep, 1, 1] + apply_cross(0, starts[sweep, 0, 0])

        if sweep == 0:

            @pl.when(jnp.logical_and(trail, later))
            def _():
                lead_map_copy(1).wait_recv()

        take_entering(sweep, 1)

        @pl.when(is_lead[1])
        def _():
            starts[sweep, 1, 0] = entering[sweep, 1]

        @pl.when(jnp.logical_and(trail, later))
        def _():
            starts[sweep, 1, 0] = starts[sweep, 1, 0] + apply_lead_map(
                1, 1, entering[sweep, 1]
            )

        middle = lower_answer + apply_half(1, 0, starts[sweep, 1, 0])
        starts[sweep, 1, 1] = middle

        @pl.when(jnp.logical_and(trail, jnp.logical_not(is_last[1])))
        def _():
            pair_out[sweep, 1] = upper_answer[...] + apply_half(1, 1, middle)
            pair_copy(sweep, 1, 1).start()
            pair_copy(sweep, 1, 0).start()

        start_copy(sweep, 1).start()

    def solve_from_start(sweep, d):
        start_tip[:, my_rows, :] = starts[sweep, d, place[d]]
        start_copy(sweep, d).wait_recv()
        start_tip[:, other_rows, :] = other_start[sweep, d]
        solve(d)

    def solve(d):
        def body(step, vector):
            w, vector = advance_line(d, step, vector)
            work[:, w] = vector
            return vector

        line_loop(0, body, start_tip[...])

    def prepare_upper():
        make_upper_maps()
        find_upper_tip(0)
        begin_upper(0)

    in_lower_half = quad < quads // 2

    loads[1].wait()
    transpose_coupling(0, low)
    pl.semaphore_wait(barrier, 4 + from_below + from_above)
    loads[0].wait()
    for copy in halo_copies(0):
        copy.start()
    make_lower_map()
    for load in loads[2:6]:
        load.wait()

    for sweep in range(SWEEPS):
        make_sources(sweep)
        find_lower_tip(sweep)
        if sweep == 0:
            loads[6].wait()
            transpose_coupling(1, upp)
        else:
            find_upper_tip(sweep)
        begin_lower(sweep)
        if sweep == 0:
            pl.when(jnp.logical_not(in_lower_half))(prepare_upper)
        else:
            begin_upper(sweep)
        finish_lower(sweep)
        if sweep == 0:
            pl.when(in_lower_half)(prepare_upper)

        @pl.when(jnp.logical_not(is_first[1]))
        def _():
            solve_from_start(sweep, 0)

        finish_upper(sweep)

        @pl.when(is_first[1])
        def _():
            solve_from_start(sweep, 0)

        solve_from_start(sweep, 1)
        last = sweep == SWEEPS - 1

        def one_variable(i, carry):
            values = jnp.swapaxes(work[i], 0, 1)
            if last:
                out_ref[i] = values
            else:
                adj[sweep + 1, i, body_rows] = values.reshape(girth * wall, stream)
            return carry

        lax.fori_loop(0, nv, one_variable, 0)
        if not last:
            for copy in halo_copies(sweep + 1):
                copy.start()

    for sweep in range(SWEEPS):
        for copy in halo_copies(sweep):
            copy.wait_send()
    cross_copy().wait_send()

    @pl.when(is_lead[1])
    def _():
        chip_cross_copy().wait_send()

    for d in range(2):
        map_copy(d).wait_send()

        @pl.when(jnp.logical_and(is_lead[d], jnp.logical_not(is_first[d])))
        def _():
            lead_map_copy(d).wait_send()

        for sweep in range(SWEEPS):
            tip_copy(sweep, d).wait_send()
            start_copy(sweep, d).wait_send()

            @pl.when(is_lead[d])
            def _():
                lead_copy(sweep, d).wait_send()

            @pl.when(jnp.logical_and(jnp.logical_not(is_lead[d]), jnp.logical_not(is_last[d])))
            def _():
                pair_copy(sweep, d, 0).wait_send()
                pair_copy(sweep, d, 1).wait_send()


def on_device(
    girth_size,
    wall_size,
    adjoint_start,
    right_side,
    pivot_inverse,
    lower_coupling,
    upper_coupling,
    girth_coeff,
    stream_coeff,
):
    nv, girth, wall, stream = adjoint_start.shape
    half = girth // HALVES
    flat = (nv, girth * wall, stream)
    blocks = (nv, nv, girth, wall, stream)
    tip = (nv, half, stream)
    half_blocks = (nv, nv, half, stream)
    dma = pltpu.SemaphoreType.DMA
    out = pl.pallas_call(
        functools.partial(kernel, girth_size, wall_size, (nv, girth, wall, stream)),
        out_shape=jax.ShapeDtypeStruct((nv, girth, wall, stream), F32),
        in_specs=[pl.BlockSpec(memory_space=pl.ANY)] * 7,
        out_specs=pl.BlockSpec(memory_space=pltpu.VMEM),
        scratch_shapes=[
            pltpu.VMEM((SWEEPS, nv, (girth + 2 * HALO) * wall, stream), F32),
            pltpu.VMEM((nv, girth, wall, stream), F32),
            pltpu.VMEM(blocks, jnp.bfloat16),
            pltpu.VMEM(blocks, jnp.bfloat16),
            pltpu.VMEM(blocks, jnp.bfloat16),
            pltpu.VMEM((nv, girth, wall, stream), jnp.bfloat16),
            pltpu.VMEM((nv, girth, wall, stream), jnp.bfloat16),
            pltpu.VMEM((2, nv, nv, wall, girth, stream), F32),
            pltpu.VMEM((nv, wall, girth, stream), F32),
            pltpu.VMEM((nv, girth, wall, stream), F32),
            pltpu.VMEM((2, *half_blocks), F32),
            pltpu.VMEM((2, 2, *half_blocks), F32),
            pltpu.VMEM((2, 2, *half_blocks), F32),
            pltpu.VMEM((nv, nv, wall, girth, stream), F32),
            pltpu.VMEM(half_blocks, F32),
            pltpu.VMEM((2, *half_blocks), F32),
            pltpu.VMEM((2, *half_blocks), F32),
            pltpu.VMEM((nv, wall, girth, stream), F32),
            pltpu.VMEM((SWEEPS, 2, *tip), F32),
            pltpu.VMEM((SWEEPS, 2, 2, *tip), F32),
            pltpu.VMEM((SWEEPS, 2, 2, *tip), F32),
            pltpu.VMEM((SWEEPS, 2, *tip), F32),
            pltpu.VMEM((SWEEPS, 2, *tip), F32),
            pltpu.VMEM((SWEEPS, 2, 2, *tip), F32),
            pltpu.VMEM((SWEEPS, 2, *tip), F32),
            pltpu.VMEM((nv, girth, stream), F32),
            pltpu.VMEM((nv, girth, stream), F32),
            pltpu.VMEM(tip, F32),
            pltpu.VMEM(tip, F32),
            dma((7,)),
            dma((SWEEPS, 2)),
            dma((SWEEPS, 2)),
            dma((2,)),
            dma((2,)),
            dma((2,)),
            dma((2,)),
            dma,
            dma,
            dma,
            dma,
            dma((SWEEPS, 2)),
            dma((SWEEPS, 2)),
            dma((SWEEPS, 2)),
            dma((SWEEPS, 2)),
            dma((SWEEPS, 2, 2)),
            dma((SWEEPS, 2)),
            dma((SWEEPS, 2)),
            dma((SWEEPS, 2)),
        ],
        compiler_params=pltpu.CompilerParams(
            collective_id=0, has_side_effects=True, vmem_limit_bytes=62 * 2**20
        ),
    )(
        adjoint_start.reshape(flat),
        right_side,
        pivot_inverse,
        lower_coupling,
        upper_coupling,
        girth_coeff,
        stream_coeff,
    )
    return out


def solution(mesh):
    in_specs = (
        P(None, "girth", "wall", None),
        P(None, "girth", "wall", None),
        P(None, None, "girth", "wall", None),
        P(None, None, "girth", "wall", None),
        P(None, None, "girth", "wall", None),
        P(None, "girth", "wall", None),
        P(None, "girth", "wall", None),
    )
    out_specs = P(None, "girth", "wall", None)
    return jax.shard_map(
        functools.partial(on_device, mesh.shape["girth"], mesh.shape["wall"]),
        mesh=mesh,
        in_specs=in_specs,
        out_specs=out_specs,
        check_vma=False,
    )
```

```python
import functools

import jax
import jax.numpy as jnp
from jax import lax
from jax.experimental import pallas as pl
from jax.experimental.pallas import tpu as pltpu
from jax.sharding import PartitionSpec as P

SWEEPS = 2
HALO = 2
HALVES = 2
MESH = pl.DeviceIdType.MESH
F32 = jnp.float32


def block_product(column, vector):
    terms = [column(j) * vector[j][None] for j in range(vector.shape[0])]
    while len(terms) > 1:
        pairs = [a + b for a, b in zip(terms[::2], terms[1::2])]
        terms = pairs + terms[len(pairs) * 2 :]
    return terms[0]


def kernel(
    girth_size,
    wall_size,
    sizes,
    adj_hbm,
    rhs_hbm,
    piv_hbm,
    low_hbm,
    upp_hbm,
    gc_hbm,
    sc_hbm,
    out_ref,
    adj,
    rhs,
    piv,
    low,
    upp,
    gc,
    sc,
    couplings,
    work,
    staged,
    other_map,
    half_map,
    lead_map,
    products,
    other_cross,
    half_cross,
    chip_cross,
    trial,
    other_tip,
    half_tip,
    lead_tip,
    pair_out,
    entering,
    starts,
    other_start,
    start_tip,
    whole_column,
    mate_start,
    upper_answer,
    load_sem,
    halo_send,
    halo_recv,
    map_send,
    map_recv,
    lead_map_send,
    lead_map_recv,
    cross_send,
    cross_recv,
    chip_cross_send,
    chip_cross_recv,
    tip_send,
    tip_recv,
    lead_send,
    lead_recv,
    pair_send,
    pair_recv,
    start_send,
    start_recv,
):
    nv, girth, wall, stream = sizes
    half = girth // HALVES
    quads = wall_size // 4
    my_girth = lax.axis_index("girth")
    my_wall = lax.axis_index("wall")
    chip = my_wall // 2
    core = lax.rem(my_wall, 2)
    quad = my_wall // 4
    side = lax.rem(chip, 2)
    right = (lax.rem(my_girth + 1, girth_size), my_wall)
    left = (lax.rem(my_girth + girth_size - 1, girth_size), my_wall)
    partner = (my_girth, chip * 2 + 1 - core)

    def on_chip(other_chip):
        return (my_girth, other_chip * 2 + core)

    place = (core, 1 - core)
    is_lead = (side == 0, side == 1)
    is_first = (quad == 0, quad == quads - 1)
    is_last = (quad == quads - 1, quad == 0)
    mate = on_chip(quad * 2 + 1 - side)
    my_rows = pl.ds(pl.multiple_of(core * half, half), half)
    other_rows = pl.ds(pl.multiple_of((1 - core) * half, half), half)

    body_rows = pl.ds(HALO * wall, girth * wall)
    loads = [
        pltpu.make_async_copy(adj_hbm, adj.at[0, :, body_rows, :], load_sem.at[0]),
        pltpu.make_async_copy(low_hbm, low, load_sem.at[1]),
        pltpu.make_async_copy(rhs_hbm, rhs, load_sem.at[2]),
        pltpu.make_async_copy(gc_hbm, gc, load_sem.at[3]),
        pltpu.make_async_copy(sc_hbm, sc, load_sem.at[4]),
        pltpu.make_async_copy(piv_hbm, piv, load_sem.at[5]),
        pltpu.make_async_copy(upp_hbm, upp, load_sem.at[6]),
    ]
    for load in loads:
        load.start()

    barrier = pltpu.get_barrier_semaphore()

    def greet(device):
        pl.semaphore_signal(barrier, inc=1, device_id=device, device_id_type=MESH)

    greet(left)
    greet(right)
    greet(partner)
    greet(mate)

    @pl.when(quad > 0)
    def _():
        greet(on_chip(chip - 2))

        @pl.when(side == 0)
        def _():
            greet(on_chip(chip - 1))

    @pl.when(quad < quads - 1)
    def _():
        greet(on_chip(chip + 2))

        @pl.when(side == 1)
        def _():
            greet(on_chip(chip + 1))

    from_below = jnp.where(quad > 0, 2 - side, 0)
    from_above = jnp.where(quad < quads - 1, 1 + side, 0)

    def remote(src, dst, send_sem, recv_sem, device):
        return pltpu.make_async_remote_copy(
            src_ref=src,
            dst_ref=dst,
            send_sem=send_sem,
            recv_sem=recv_sem,
            device_id=device,
            device_id_type=MESH,
        )

    def halo_copies(sweep):
        field = adj.at[sweep]
        width = HALO * wall
        return [
            remote(
                field.at[:, pl.ds(width, width), :],
                field.at[:, pl.ds(width + girth * wall, width), :],
                halo_send.at[sweep, 0],
                halo_recv.at[sweep, 0],
                left,
            ),
            remote(
                field.at[:, pl.ds(girth * wall, width), :],
                field.at[:, pl.ds(0, width), :],
                halo_send.at[sweep, 1],
                halo_recv.at[sweep, 1],
                right,
            ),
        ]

    def coupling_column(d, w):
        return lambda j: couplings[d, :, j, w]

    def line_loop(begin, body, carry):
        return lax.fori_loop(begin, wall, body, carry)

    def order(d, step):
        return step if d == 0 else wall - 1 - step

    def transpose_coupling(d, source):
        def one_row(i, carry):
            def one_block(j, inner):
                couplings[d, i, j] = jnp.swapaxes(source[i, j].astype(F32), 0, 1)
                return inner

            return lax.fori_loop(0, nv, one_block, carry)

        lax.fori_loop(0, nv, one_row, 0)

    def map_copy(d):
        return remote(
            other_map.at[d], half_map.at[d, place[d]], map_send.at[d], map_recv.at[d], partner
        )

    def keep_halves(column, half_ref, other_ref, k):
        whole_column[...] = column
        half_ref[:, k] = whole_column[:, my_rows, :]
        other_ref[:, k] = whole_column[:, other_rows, :]

    def make_lower_map():
        first = coupling_column(0, 0)
        def two_columns(pair, carry):
            k = 2 * pair

            def advance(w, columns):
                column = coupling_column(0, w)
                columns = tuple(block_product(column, c) for c in columns)
                products[:, k, w] = columns[0]
                products[:, k + 1, w] = columns[1]
                return columns

            products[:, k, 0] = first(k)
            products[:, k + 1, 0] = first(k + 1)
            columns = line_loop(1, advance, (first(k), first(k + 1)))
            for shift in range(2):
                keep_halves(
                    columns[shift], half_map.at[0, place[0]], other_map.at[0], k + shift
                )
            return carry

        lax.fori_loop(0, nv // 2, two_columns, 0)
        map_copy(0).start()

    def cross_copy():
        return remote(
            other_cross, half_cross.at[core], cross_send, cross_recv, partner
        )

    def chip_cross_copy():
        return remote(
            chip_cross.at[0], chip_cross.at[1], chip_cross_send, chip_cross_recv, mate
        )

    def make_upper_maps():
        first = coupling_column(1, wall - 1)
        def one_column(k, carry):

            def advance(step, columns):
                w = order(1, step)
                column = coupling_column(1, w)
                return (
                    block_product(column, columns[0]),
                    products[:, k, w] + block_product(column, columns[1]),
                )

            columns = line_loop(1, advance, (first(k), products[:, k, wall - 1]))
            keep_halves(columns[0], half_map.at[1, place[1]], other_map.at[1], k)
            keep_halves(columns[1], half_cross.at[core], other_cross, k)
            return carry

        lax.fori_loop(0, nv, one_column, 0)
        map_copy(1).start()
        cross_copy().start()

    def make_chip_cross():
        @pl.when(is_lead[1])
        def _():
            def one_column(k, carry):
                column = block_product(lambda j: half_cross[1, :, j], half_map[0, 0, :, k])
                column = apply_half(1, 1, column)
                chip_cross[0, :, k] = half_cross[0, :, k] + column
                return carry

            lax.fori_loop(0, nv, one_column, 0)
            chip_cross_copy().start()

    def lead_map_copy(d):
        return remote(
            lead_map.at[d, 0], lead_map.at[d, 1], lead_map_send.at[d], lead_map_recv.at[d], mate
        )

    def make_lead_map(d):
        @pl.when(jnp.logical_and(is_lead[d], jnp.logical_not(is_first[d])))
        def _():
            def one_column(k, carry):
                lead_map[d, 0, :, k] = block_product(
                    lambda j: half_map[d, 1, :, j], half_map[d, 0, :, k]
                )
                return carry

            lax.fori_loop(0, nv, one_column, 0)
            lead_map_copy(d).start()

    lane = lax.broadcasted_iota(jnp.int32, (nv, wall, stream), 2)

    def make_source(sweep, g):
        def girth_layer(offset):
            rows = pl.ds(pl.multiple_of((g + HALO + offset) * wall, wall), wall)
            return adj[sweep, :, rows, :]

        here = girth_layer(0)
        beside_pair = girth_layer(-1) + girth_layer(1)
        distant_pair = girth_layer(-2) + girth_layer(2)
        before = jnp.where(lane == 0, 0.0, pltpu.roll(here, 1, 2))
        after = jnp.where(lane == stream - 1, 0.0, pltpu.roll(here, stream - 1, 2))
        neighbours = gc[:, g].astype(F32) * (beside_pair - 0.25 * distant_pair) + sc[
            :, g
        ].astype(F32) * (before + after)
        loaded = rhs[:, g] + neighbours
        staged[:, g] = block_product(
            lambda j: piv[:, j, g].astype(F32), loaded
        )

    def make_sources(sweep):
        def body(g, carry):
            make_source(sweep, g)
            return carry

        lax.fori_loop(HALO, girth - HALO, body, 0)
        for copy in halo_copies(sweep):
            copy.wait_recv()
        lax.fori_loop(0, HALO, body, 0)
        lax.fori_loop(girth - HALO, girth, body, 0)

        def one_variable(i, carry):
            work[i] = jnp.swapaxes(staged[i], 0, 1)
            return carry

        lax.fori_loop(0, nv, one_variable, 0)

    def advance_line(d, step, vector):
        w = order(d, step)
        return w, work[:, w] + block_product(coupling_column(d, w), vector)

    def send_tip(sweep, d, tip):
        whole_column[...] = tip
        half_tip[sweep, d, place[d]] = whole_column[:, my_rows, :]
        other_tip[sweep, d] = whole_column[:, other_rows, :]
        tip_copy(sweep, d).start()

    def find_lower_tip(sweep):
        def body(w, vector):
            vector = advance_line(0, w, vector)[1]
            trial[:, w] = vector
            return vector

        trial[:, 0] = work[:, 0]
        send_tip(sweep, 0, line_loop(1, body, work[:, 0]))

    def find_upper_tip(sweep):
        def body(step, vector):
            w = order(1, step)
            return trial[:, w] + block_product(coupling_column(1, w), vector)

        send_tip(sweep, 1, line_loop(1, body, trial[:, wall - 1]))

    def tip_copy(sweep, d):
        return remote(
            other_tip.at[sweep, d],
            half_tip.at[sweep, d, place[d]],
            tip_send.at[sweep, d],
            tip_recv.at[sweep, d],
            partner,
        )

    def lead_copy(sweep, d):
        return remote(
            lead_tip.at[sweep, d, 0],
            lead_tip.at[sweep, d, 1],
            lead_send.at[sweep, d],
            lead_recv.at[sweep, d],
            mate,
        )

    def pair_copy(sweep, d, target):
        sign = 1 if d == 0 else -1
        return remote(
            pair_out.at[sweep, d],
            entering.at[sweep, d],
            pair_send.at[sweep, d, target],
            pair_recv.at[sweep, d],
            on_chip(chip + sign * (target + 1)),
        )

    def start_copy(sweep, d):
        return remote(
            starts.at[sweep, d, 1 - place[d]],
            other_start.at[sweep, d],
            start_send.at[sweep, d],
            start_recv.at[sweep, d],
            partner,
        )

    def apply_half(d, which, vector):
        return block_product(lambda j: half_map[d, which, :, j], vector)

    def apply_cross(which, vector):
        return block_product(lambda j: half_cross[which, :, j], vector)

    def begin_lower(sweep):
        if sweep == 0:
            map_copy(0).wait_recv()
        tip_copy(sweep, 0).wait_recv()

        @pl.when(is_lead[0])
        def _():
            lead_tip[sweep, 0, 0] = half_tip[sweep, 0, 1] + apply_half(
                0, 1, half_tip[sweep, 0, 0]
            )
            lead_copy(sweep, 0).start()

        if sweep == 0:
            make_lead_map(0)

    def begin_upper(sweep):
        if sweep == 0:
            map_copy(1).wait_recv()
            cross_copy().wait_recv()
        tip_copy(sweep, 1).wait_recv()

        @pl.when(is_lead[1])
        def _():
            reached = half_tip[sweep, 1, 0] + apply_cross(1, half_tip[sweep, 0, 0])
            lead_tip[sweep, 1, 0] = half_tip[sweep, 1, 1] + apply_half(1, 1, reached)
            lead_copy(sweep, 1).start()

        if sweep == 0:
            make_chip_cross()
            make_lead_map(1)

    def take_entering(sweep, d):
        @pl.when(is_first[d])
        def _():
            entering[sweep, d] = jnp.zeros_like(entering[sweep, d])

        @pl.when(jnp.logical_not(is_first[d]))
        def _():
            pair_copy(sweep, d, 0).wait_recv()

    def apply_lead_map(d, which, vector):
        return block_product(lambda j: lead_map[d, which, :, j], vector)

    def finish_lower(sweep):
        later = jnp.logical_not(is_first[0])
        trail = jnp.logical_not(is_lead[0])

        @pl.when(trail)
        def _():
            lead_copy(sweep, 0).wait_recv()

        if sweep == 0:

            @pl.when(jnp.logical_and(trail, later))
            def _():
                lead_map_copy(0).wait_recv()

        take_entering(sweep, 0)

        @pl.when(is_lead[0])
        def _():
            starts[sweep, 0, 0] = entering[sweep, 0]

        @pl.when(jnp.logical_and(trail, is_first[0]))
        def _():
            starts[sweep, 0, 0] = lead_tip[sweep, 0, 1]

        @pl.when(jnp.logical_and(trail, later))
        def _():
            starts[sweep, 0, 0] = lead_tip[sweep, 0, 1] + apply_lead_map(
                0, 1, entering[sweep, 0]
            )

        middle = half_tip[sweep, 0, 0] + apply_half(0, 0, starts[sweep, 0, 0])
        starts[sweep, 0, 1] = middle

        @pl.when(jnp.logical_and(trail, jnp.logical_not(is_last[0])))
        def _():
            pair_out[sweep, 0] = half_tip[sweep, 0, 1] + apply_half(0, 1, middle)
            pair_copy(sweep, 0, 1).start()
            pair_copy(sweep, 0, 0).start()

        start_copy(sweep, 0).start()

    def finish_upper(sweep):
        later = jnp.logical_not(is_first[1])
        trail = jnp.logical_not(is_lead[1])

        @pl.when(trail)
        def _():
            lead_copy(sweep, 1).wait_recv()
            if sweep == 0:
                chip_cross_copy().wait_recv()
            mate_start[...] = lead_tip[sweep, 0, 0]

        @pl.when(jnp.logical_and(trail, jnp.logical_not(is_first[0])))
        def _():
            mate_start[...] = mate_start[...] + apply_lead_map(0, 0, entering[sweep, 0])

        @pl.when(trail)
        def _():
            starts[sweep, 1, 0] = lead_tip[sweep, 1, 1] + block_product(
                lambda j: chip_cross[1, :, j], mate_start[...]
            )

        lower_answer = half_tip[sweep, 1, 0] + apply_cross(1, starts[sweep, 0, 1])
        upper_answer[...] = half_tip[sweep, 1, 1] + apply_cross(0, starts[sweep, 0, 0])

        if sweep == 0:

            @pl.when(jnp.logical_and(trail, later))
            def _():
                lead_map_copy(1).wait_recv()

        take_entering(sweep, 1)

        @pl.when(is_lead[1])
        def _():
            starts[sweep, 1, 0] = entering[sweep, 1]

        @pl.when(jnp.logical_and(trail, later))
        def _():
            starts[sweep, 1, 0] = starts[sweep, 1, 0] + apply_lead_map(
                1, 1, entering[sweep, 1]
            )

        middle = lower_answer + apply_half(1, 0, starts[sweep, 1, 0])
        starts[sweep, 1, 1] = middle

        @pl.when(jnp.logical_and(trail, jnp.logical_not(is_last[1])))
        def _():
            pair_out[sweep, 1] = upper_answer[...] + apply_half(1, 1, middle)
            pair_copy(sweep, 1, 1).start()
            pair_copy(sweep, 1, 0).start()

        start_copy(sweep, 1).start()

    def solve_from_start(sweep, d):
        start_tip[:, my_rows, :] = starts[sweep, d, place[d]]
        start_copy(sweep, d).wait_recv()
        start_tip[:, other_rows, :] = other_start[sweep, d]
        solve(d)

    def solve(d):
        def body(step, vector):
            w, vector = advance_line(d, step, vector)
            work[:, w] = vector
            return vector

        line_loop(0, body, start_tip[...])

    def prepare_upper():
        make_upper_maps()
        find_upper_tip(0)
        begin_upper(0)

    in_lower_half = quad < quads // 2

    loads[1].wait()
    transpose_coupling(0, low)
    pl.semaphore_wait(barrier, 4 + from_below + from_above)
    loads[0].wait()
    for copy in halo_copies(0):
        copy.start()
    make_lower_map()
    for load in loads[2:6]:
        load.wait()

    for sweep in range(SWEEPS):
        make_sources(sweep)
        find_lower_tip(sweep)
        if sweep == 0:
            loads[6].wait()
            transpose_coupling(1, upp)
        else:
            find_upper_tip(sweep)
        begin_lower(sweep)
        if sweep == 0:
            pl.when(in_lower_half)(functools.partial(finish_lower, 0))
            prepare_upper()
            pl.when(jnp.logical_not(in_lower_half))(functools.partial(finish_lower, 0))
        else:
            begin_upper(sweep)
            finish_lower(sweep)

        @pl.when(jnp.logical_not(is_first[1]))
        def _():
            solve_from_start(sweep, 0)

        finish_upper(sweep)

        @pl.when(is_first[1])
        def _():
            solve_from_start(sweep, 0)

        solve_from_start(sweep, 1)
        last = sweep == SWEEPS - 1

        def one_variable(i, carry):
            values = jnp.swapaxes(work[i], 0, 1)
            if last:
                out_ref[i] = values
            else:
                adj[sweep + 1, i, body_rows] = values.reshape(girth * wall, stream)
            return carry

        lax.fori_loop(0, nv, one_variable, 0)
        if not last:
            for copy in halo_copies(sweep + 1):
                copy.start()

    for sweep in range(SWEEPS):
        for copy in halo_copies(sweep):
            copy.wait_send()
    cross_copy().wait_send()

    @pl.when(is_lead[1])
    def _():
        chip_cross_copy().wait_send()

    for d in range(2):
        map_copy(d).wait_send()

        @pl.when(jnp.logical_and(is_lead[d], jnp.logical_not(is_first[d])))
        def _():
            lead_map_copy(d).wait_send()

        for sweep in range(SWEEPS):
            tip_copy(sweep, d).wait_send()
            start_copy(sweep, d).wait_send()

            @pl.when(is_lead[d])
            def _():
                lead_copy(sweep, d).wait_send()

            @pl.when(jnp.logical_and(jnp.logical_not(is_lead[d]), jnp.logical_not(is_last[d])))
            def _():
                pair_copy(sweep, d, 0).wait_send()
                pair_copy(sweep, d, 1).wait_send()


def on_device(
    girth_size,
    wall_size,
    adjoint_start,
    right_side,
    pivot_inverse,
    lower_coupling,
    upper_coupling,
    girth_coeff,
    stream_coeff,
):
    nv, girth, wall, stream = adjoint_start.shape
    half = girth // HALVES
    flat = (nv, girth * wall, stream)
    blocks = (nv, nv, girth, wall, stream)
    tip = (nv, half, stream)
    half_blocks = (nv, nv, half, stream)
    dma = pltpu.SemaphoreType.DMA
    out = pl.pallas_call(
        functools.partial(kernel, girth_size, wall_size, (nv, girth, wall, stream)),
        out_shape=jax.ShapeDtypeStruct((nv, girth, wall, stream), F32),
        in_specs=[pl.BlockSpec(memory_space=pl.ANY)] * 7,
        out_specs=pl.BlockSpec(memory_space=pltpu.VMEM),
        scratch_shapes=[
            pltpu.VMEM((SWEEPS, nv, (girth + 2 * HALO) * wall, stream), F32),
            pltpu.VMEM((nv, girth, wall, stream), F32),
            pltpu.VMEM(blocks, jnp.bfloat16),
            pltpu.VMEM(blocks, jnp.bfloat16),
            pltpu.VMEM(blocks, jnp.bfloat16),
            pltpu.VMEM((nv, girth, wall, stream), jnp.bfloat16),
            pltpu.VMEM((nv, girth, wall, stream), jnp.bfloat16),
            pltpu.VMEM((2, nv, nv, wall, girth, stream), F32),
            pltpu.VMEM((nv, wall, girth, stream), F32),
            pltpu.VMEM((nv, girth, wall, stream), F32),
            pltpu.VMEM((2, *half_blocks), F32),
            pltpu.VMEM((2, 2, *half_blocks), F32),
            pltpu.VMEM((2, 2, *half_blocks), F32),
            pltpu.VMEM((nv, nv, wall, girth, stream), F32),
            pltpu.VMEM(half_blocks, F32),
            pltpu.VMEM((2, *half_blocks), F32),
            pltpu.VMEM((2, *half_blocks), F32),
            pltpu.VMEM((nv, wall, girth, stream), F32),
            pltpu.VMEM((SWEEPS, 2, *tip), F32),
            pltpu.VMEM((SWEEPS, 2, 2, *tip), F32),
            pltpu.VMEM((SWEEPS, 2, 2, *tip), F32),
            pltpu.VMEM((SWEEPS, 2, *tip), F32),
            pltpu.VMEM((SWEEPS, 2, *tip), F32),
            pltpu.VMEM((SWEEPS, 2, 2, *tip), F32),
            pltpu.VMEM((SWEEPS, 2, *tip), F32),
            pltpu.VMEM((nv, girth, stream), F32),
            pltpu.VMEM((nv, girth, stream), F32),
            pltpu.VMEM(tip, F32),
            pltpu.VMEM(tip, F32),
            dma((7,)),
            dma((SWEEPS, 2)),
            dma((SWEEPS, 2)),
            dma((2,)),
            dma((2,)),
            dma((2,)),
            dma((2,)),
            dma,
            dma,
            dma,
            dma,
            dma((SWEEPS, 2)),
            dma((SWEEPS, 2)),
            dma((SWEEPS, 2)),
            dma((SWEEPS, 2)),
            dma((SWEEPS, 2, 2)),
            dma((SWEEPS, 2)),
            dma((SWEEPS, 2)),
            dma((SWEEPS, 2)),
        ],
        compiler_params=pltpu.CompilerParams(
            collective_id=0, has_side_effects=True, vmem_limit_bytes=62 * 2**20
        ),
    )(
        adjoint_start.reshape(flat),
        right_side,
        pivot_inverse,
        lower_coupling,
        upper_coupling,
        girth_coeff,
        stream_coeff,
    )
    return out


def solution(mesh):
    in_specs = (
        P(None, "girth", "wall", None),
        P(None, "girth", "wall", None),
        P(None, None, "girth", "wall", None),
        P(None, None, "girth", "wall", None),
        P(None, None, "girth", "wall", None),
        P(None, "girth", "wall", None),
        P(None, "girth", "wall", None),
    )
    out_specs = P(None, "girth", "wall", None)
    return jax.shard_map(
        functools.partial(on_device, mesh.shape["girth"], mesh.shape["wall"]),
        mesh=mesh,
        in_specs=in_specs,
        out_specs=out_specs,
        check_vma=False,
    )
```

```python
import functools

import jax
import jax.numpy as jnp
from jax import lax
from jax.experimental import pallas as pl
from jax.experimental.pallas import tpu as pltpu
from jax.sharding import PartitionSpec as P

SWEEPS = 2
HALO = 2
HALVES = 2
MESH = pl.DeviceIdType.MESH
F32 = jnp.float32


def block_product(column, vector):
    total = column(0) * vector[0][None]
    for j in range(1, vector.shape[0]):
        total = total + column(j) * vector[j][None]
    return total


def kernel(
    girth_size,
    wall_size,
    sizes,
    adj_hbm,
    rhs_hbm,
    piv_hbm,
    low_hbm,
    upp_hbm,
    gc_hbm,
    sc_hbm,
    out_ref,
    adj,
    rhs,
    piv,
    low,
    upp,
    gc,
    sc,
    couplings,
    work,
    staged,
    other_map,
    half_map,
    lead_map,
    products,
    other_cross,
    half_cross,
    chip_cross,
    trial,
    other_tip,
    half_tip,
    lead_tip,
    pair_out,
    entering,
    starts,
    other_start,
    start_tip,
    whole_column,
    mate_start,
    upper_answer,
    load_sem,
    halo_send,
    halo_recv,
    map_send,
    map_recv,
    lead_map_send,
    lead_map_recv,
    cross_send,
    cross_recv,
    chip_cross_send,
    chip_cross_recv,
    tip_send,
    tip_recv,
    lead_send,
    lead_recv,
    pair_send,
    pair_recv,
    start_send,
    start_recv,
):
    nv, girth, wall, stream = sizes
    half = girth // HALVES
    quads = wall_size // 4
    my_girth = lax.axis_index("girth")
    my_wall = lax.axis_index("wall")
    chip = my_wall // 2
    core = lax.rem(my_wall, 2)
    quad = my_wall // 4
    side = lax.rem(chip, 2)
    right = (lax.rem(my_girth + 1, girth_size), my_wall)
    left = (lax.rem(my_girth + girth_size - 1, girth_size), my_wall)
    partner = (my_girth, chip * 2 + 1 - core)

    def on_chip(other_chip):
        return (my_girth, other_chip * 2 + core)

    place = (core, 1 - core)
    is_lead = (side == 0, side == 1)
    is_first = (quad == 0, quad == quads - 1)
    is_last = (quad == quads - 1, quad == 0)
    mate = on_chip(quad * 2 + 1 - side)
    my_rows = pl.ds(pl.multiple_of(core * half, half), half)
    other_rows = pl.ds(pl.multiple_of((1 - core) * half, half), half)

    body_rows = pl.ds(HALO * wall, girth * wall)
    loads = [
        pltpu.make_async_copy(adj_hbm, adj.at[0, :, body_rows, :], load_sem.at[0]),
        pltpu.make_async_copy(low_hbm, low, load_sem.at[1]),
        pltpu.make_async_copy(rhs_hbm, rhs, load_sem.at[2]),
        pltpu.make_async_copy(gc_hbm, gc, load_sem.at[3]),
        pltpu.make_async_copy(sc_hbm, sc, load_sem.at[4]),
        pltpu.make_async_copy(piv_hbm, piv, load_sem.at[5]),
        pltpu.make_async_copy(upp_hbm, upp, load_sem.at[6]),
    ]
    for load in loads:
        load.start()

    barrier = pltpu.get_barrier_semaphore()

    def greet(device):
        pl.semaphore_signal(barrier, inc=1, device_id=device, device_id_type=MESH)

    greet(left)
    greet(right)
    greet(partner)
    greet(mate)

    @pl.when(quad > 0)
    def _():
        greet(on_chip(chip - 2))

        @pl.when(side == 0)
        def _():
            greet(on_chip(chip - 1))

    @pl.when(quad < quads - 1)
    def _():
        greet(on_chip(chip + 2))

        @pl.when(side == 1)
        def _():
            greet(on_chip(chip + 1))

    from_below = jnp.where(quad > 0, 2 - side, 0)
    from_above = jnp.where(quad < quads - 1, 1 + side, 0)

    def remote(src, dst, send_sem, recv_sem, device):
        return pltpu.make_async_remote_copy(
            src_ref=src,
            dst_ref=dst,
            send_sem=send_sem,
            recv_sem=recv_sem,
            device_id=device,
            device_id_type=MESH,
        )

    def halo_copies(sweep):
        field = adj.at[sweep]
        width = HALO * wall
        return [
            remote(
                field.at[:, pl.ds(width, width), :],
                field.at[:, pl.ds(width + girth * wall, width), :],
                halo_send.at[sweep, 0],
                halo_recv.at[sweep, 0],
                left,
            ),
            remote(
                field.at[:, pl.ds(girth * wall, width), :],
                field.at[:, pl.ds(0, width), :],
                halo_send.at[sweep, 1],
                halo_recv.at[sweep, 1],
                right,
            ),
        ]

    def coupling_column(d, w):
        return lambda j: couplings[d, :, j, w]

    def line_loop(begin, body, carry):
        return lax.fori_loop(begin, wall, body, carry, unroll=5 if begin else 4)

    def order(d, step):
        return step if d == 0 else wall - 1 - step

    def transpose_coupling(d, source):
        def one_row(i, carry):
            for j in range(nv):
                couplings[d, i, j] = jnp.swapaxes(source[i, j].astype(F32), 0, 1)
            return carry

        lax.fori_loop(0, nv, one_row, 0)

    def map_copy(d):
        return remote(
            other_map.at[d], half_map.at[d, place[d]], map_send.at[d], map_recv.at[d], partner
        )

    def keep_halves(column, half_ref, other_ref, k):
        whole_column[...] = column
        half_ref[:, k] = whole_column[:, my_rows, :]
        other_ref[:, k] = whole_column[:, other_rows, :]

    def make_lower_map():
        first = coupling_column(0, 0)
        def two_columns(pair, carry):
            k = 2 * pair

            def advance(w, columns):
                column = coupling_column(0, w)
                columns = tuple(block_product(column, c) for c in columns)
                products[:, k, w] = columns[0]
                products[:, k + 1, w] = columns[1]
                return columns

            products[:, k, 0] = first(k)
            products[:, k + 1, 0] = first(k + 1)
            columns = line_loop(1, advance, (first(k), first(k + 1)))
            for shift in range(2):
                keep_halves(
                    columns[shift], half_map.at[0, place[0]], other_map.at[0], k + shift
                )
            return carry

        lax.fori_loop(0, nv // 2, two_columns, 0)
        map_copy(0).start()

    def cross_copy():
        return remote(
            other_cross, half_cross.at[core], cross_send, cross_recv, partner
        )

    def chip_cross_copy():
        return remote(
            chip_cross.at[0], chip_cross.at[1], chip_cross_send, chip_cross_recv, mate
        )

    def make_upper_maps():
        first = coupling_column(1, wall - 1)
        def one_column(k, carry):

            def advance(step, columns):
                w = order(1, step)
                column = coupling_column(1, w)
                return (
                    block_product(column, columns[0]),
                    products[:, k, w] + block_product(column, columns[1]),
                )

            columns = line_loop(1, advance, (first(k), products[:, k, wall - 1]))
            keep_halves(columns[0], half_map.at[1, place[1]], other_map.at[1], k)
            keep_halves(columns[1], half_cross.at[core], other_cross, k)
            return carry

        lax.fori_loop(0, nv, one_column, 0)
        map_copy(1).start()
        cross_copy().start()

    def make_chip_cross():
        @pl.when(is_lead[1])
        def _():
            def one_column(k, carry):
                column = block_product(lambda j: half_cross[1, :, j], half_map[0, 0, :, k])
                column = apply_half(1, 1, column)
                chip_cross[0, :, k] = half_cross[0, :, k] + column
                return carry

            lax.fori_loop(0, nv, one_column, 0)
            chip_cross_copy().start()

    def lead_map_copy(d):
        return remote(
            lead_map.at[d, 0], lead_map.at[d, 1], lead_map_send.at[d], lead_map_recv.at[d], mate
        )

    def make_lead_map(d):
        @pl.when(jnp.logical_and(is_lead[d], jnp.logical_not(is_first[d])))
        def _():
            def one_column(k, carry):
                lead_map[d, 0, :, k] = block_product(
                    lambda j: half_map[d, 1, :, j], half_map[d, 0, :, k]
                )
                return carry

            lax.fori_loop(0, nv, one_column, 0)
            lead_map_copy(d).start()

    lane = lax.broadcasted_iota(jnp.int32, (nv, wall, stream), 2)

    def make_source(sweep, g):
        def girth_layer(offset):
            rows = pl.ds(pl.multiple_of((g + HALO + offset) * wall, wall), wall)
            return adj[sweep, :, rows, :]

        here = girth_layer(0)
        beside_pair = girth_layer(-1) + girth_layer(1)
        distant_pair = girth_layer(-2) + girth_layer(2)
        before = jnp.where(lane == 0, 0.0, pltpu.roll(here, 1, 2))
        after = jnp.where(lane == stream - 1, 0.0, pltpu.roll(here, stream - 1, 2))
        neighbours = gc[:, g].astype(F32) * (beside_pair - 0.25 * distant_pair) + sc[
            :, g
        ].astype(F32) * (before + after)
        loaded = rhs[:, g] + neighbours
        staged[:, g] = block_product(
            lambda j: piv[:, j, g].astype(F32), loaded
        )

    def make_sources(sweep):
        def body(g, carry):
            make_source(sweep, g)
            return carry

        lax.fori_loop(HALO, girth - HALO, body, 0)
        for copy in halo_copies(sweep):
            copy.wait_recv()
        lax.fori_loop(0, HALO, body, 0)
        lax.fori_loop(girth - HALO, girth, body, 0)

        def one_variable(i, carry):
            work[i] = jnp.swapaxes(staged[i], 0, 1)
            return carry

        lax.fori_loop(0, nv, one_variable, 0)

    def advance_line(d, step, vector):
        w = order(d, step)
        return w, work[:, w] + block_product(coupling_column(d, w), vector)

    def send_tip(sweep, d, tip):
        whole_column[...] = tip
        half_tip[sweep, d, place[d]] = whole_column[:, my_rows, :]
        other_tip[sweep, d] = whole_column[:, other_rows, :]
        tip_copy(sweep, d).start()

    def find_lower_tip(sweep):
        def body(w, vector):
            vector = advance_line(0, w, vector)[1]
            trial[:, w] = vector
            return vector

        trial[:, 0] = work[:, 0]
        send_tip(sweep, 0, line_loop(1, body, work[:, 0]))

    def find_upper_tip(sweep):
        def body(step, vector):
            w = order(1, step)
            return trial[:, w] + block_product(coupling_column(1, w), vector)

        send_tip(sweep, 1, line_loop(1, body, trial[:, wall - 1]))

    def tip_copy(sweep, d):
        return remote(
            other_tip.at[sweep, d],
            half_tip.at[sweep, d, place[d]],
            tip_send.at[sweep, d],
            tip_recv.at[sweep, d],
            partner,
        )

    def lead_copy(sweep, d):
        return remote(
            lead_tip.at[sweep, d, 0],
            lead_tip.at[sweep, d, 1],
            lead_send.at[sweep, d],
            lead_recv.at[sweep, d],
            mate,
        )

    def pair_copy(sweep, d, target):
        sign = 1 if d == 0 else -1
        return remote(
            pair_out.at[sweep, d],
            entering.at[sweep, d],
            pair_send.at[sweep, d, target],
            pair_recv.at[sweep, d],
            on_chip(chip + sign * (target + 1)),
        )

    def start_copy(sweep, d):
        return remote(
            starts.at[sweep, d, 1 - place[d]],
            other_start.at[sweep, d],
            start_send.at[sweep, d],
            start_recv.at[sweep, d],
            partner,
        )

    def apply_half(d, which, vector):
        return block_product(lambda j: half_map[d, which, :, j], vector)

    def apply_cross(which, vector):
        return block_product(lambda j: half_cross[which, :, j], vector)

    def begin_lower(sweep):
        if sweep == 0:
            map_copy(0).wait_recv()
        tip_copy(sweep, 0).wait_recv()

        @pl.when(is_lead[0])
        def _():
            lead_tip[sweep, 0, 0] = half_tip[sweep, 0, 1] + apply_half(
                0, 1, half_tip[sweep, 0, 0]
            )
            lead_copy(sweep, 0).start()

        if sweep == 0:
            make_lead_map(0)

    def begin_upper(sweep):
        if sweep == 0:
            map_copy(1).wait_recv()
            cross_copy().wait_recv()
        tip_copy(sweep, 1).wait_recv()

        @pl.when(is_lead[1])
        def _():
            reached = half_tip[sweep, 1, 0] + apply_cross(1, half_tip[sweep, 0, 0])
            lead_tip[sweep, 1, 0] = half_tip[sweep, 1, 1] + apply_half(1, 1, reached)
            lead_copy(sweep, 1).start()

        if sweep == 0:
            make_chip_cross()
            make_lead_map(1)

    def take_entering(sweep, d):
        @pl.when(is_first[d])
        def _():
            entering[sweep, d] = jnp.zeros_like(entering[sweep, d])

        @pl.when(jnp.logical_not(is_first[d]))
        def _():
            pair_copy(sweep, d, 0).wait_recv()

    def apply_lead_map(d, which, vector):
        return block_product(lambda j: lead_map[d, which, :, j], vector)

    def finish_lower(sweep):
        later = jnp.logical_not(is_first[0])
        trail = jnp.logical_not(is_lead[0])

        @pl.when(trail)
        def _():
            lead_copy(sweep, 0).wait_recv()

        if sweep == 0:

            @pl.when(jnp.logical_and(trail, later))
            def _():
                lead_map_copy(0).wait_recv()

        take_entering(sweep, 0)

        @pl.when(is_lead[0])
        def _():
            starts[sweep, 0, 0] = entering[sweep, 0]

        @pl.when(jnp.logical_and(trail, is_first[0]))
        def _():
            starts[sweep, 0, 0] = lead_tip[sweep, 0, 1]

        @pl.when(jnp.logical_and(trail, later))
        def _():
            starts[sweep, 0, 0] = lead_tip[sweep, 0, 1] + apply_lead_map(
                0, 1, entering[sweep, 0]
            )

        middle = half_tip[sweep, 0, 0] + apply_half(0, 0, starts[sweep, 0, 0])
        starts[sweep, 0, 1] = middle

        @pl.when(jnp.logical_and(trail, jnp.logical_not(is_last[0])))
        def _():
            pair_out[sweep, 0] = half_tip[sweep, 0, 1] + apply_half(0, 1, middle)
            pair_copy(sweep, 0, 1).start()
            pair_copy(sweep, 0, 0).start()

        start_copy(sweep, 0).start()

    def finish_upper(sweep):
        later = jnp.logical_not(is_first[1])
        trail = jnp.logical_not(is_lead[1])

        @pl.when(trail)
        def _():
            lead_copy(sweep, 1).wait_recv()
            if sweep == 0:
                chip_cross_copy().wait_recv()
            mate_start[...] = lead_tip[sweep, 0, 0]

        @pl.when(jnp.logical_and(trail, jnp.logical_not(is_first[0])))
        def _():
            mate_start[...] = mate_start[...] + apply_lead_map(0, 0, entering[sweep, 0])

        @pl.when(trail)
        def _():
            starts[sweep, 1, 0] = lead_tip[sweep, 1, 1] + block_product(
                lambda j: chip_cross[1, :, j], mate_start[...]
            )

        lower_answer = half_tip[sweep, 1, 0] + apply_cross(1, starts[sweep, 0, 1])
        upper_answer[...] = half_tip[sweep, 1, 1] + apply_cross(0, starts[sweep, 0, 0])

        if sweep == 0:

            @pl.when(jnp.logical_and(trail, later))
            def _():
                lead_map_copy(1).wait_recv()

        take_entering(sweep, 1)

        @pl.when(is_lead[1])
        def _():
            starts[sweep, 1, 0] = entering[sweep, 1]

        @pl.when(jnp.logical_and(trail, later))
        def _():
            starts[sweep, 1, 0] = starts[sweep, 1, 0] + apply_lead_map(
                1, 1, entering[sweep, 1]
            )

        middle = lower_answer + apply_half(1, 0, starts[sweep, 1, 0])
        starts[sweep, 1, 1] = middle

        @pl.when(jnp.logical_and(trail, jnp.logical_not(is_last[1])))
        def _():
            pair_out[sweep, 1] = upper_answer[...] + apply_half(1, 1, middle)
            pair_copy(sweep, 1, 1).start()
            pair_copy(sweep, 1, 0).start()

        start_copy(sweep, 1).start()

    def solve_from_start(sweep, d):
        start_tip[:, my_rows, :] = starts[sweep, d, place[d]]
        start_copy(sweep, d).wait_recv()
        start_tip[:, other_rows, :] = other_start[sweep, d]
        solve(d)

    def solve(d):
        def body(step, vector):
            w, vector = advance_line(d, step, vector)
            work[:, w] = vector
            return vector

        line_loop(0, body, start_tip[...])

    def prepare_upper():
        make_upper_maps()
        find_upper_tip(0)
        begin_upper(0)

    in_lower_half = quad < quads // 2

    loads[1].wait()
    transpose_coupling(0, low)
    pl.semaphore_wait(barrier, 4 + from_below + from_above)
    loads[0].wait()
    for copy in halo_copies(0):
        copy.start()
    make_lower_map()
    for load in loads[2:6]:
        load.wait()

    for sweep in range(SWEEPS):
        make_sources(sweep)
        find_lower_tip(sweep)
        if sweep == 0:
            loads[6].wait()
            transpose_coupling(1, upp)
        else:
            find_upper_tip(sweep)
        begin_lower(sweep)
        if sweep == 0:
            pl.when(in_lower_half)(functools.partial(finish_lower, 0))
            prepare_upper()
            pl.when(jnp.logical_not(in_lower_half))(functools.partial(finish_lower, 0))
        else:
            begin_upper(sweep)
            finish_lower(sweep)

        @pl.when(jnp.logical_not(is_first[1]))
        def _():
            solve_from_start(sweep, 0)

        finish_upper(sweep)

        @pl.when(is_first[1])
        def _():
            solve_from_start(sweep, 0)

        solve_from_start(sweep, 1)
        last = sweep == SWEEPS - 1

        def one_variable(i, carry):
            values = jnp.swapaxes(work[i], 0, 1)
            if last:
                out_ref[i] = values
            else:
                adj[sweep + 1, i, body_rows] = values.reshape(girth * wall, stream)
            return carry

        lax.fori_loop(0, nv, one_variable, 0)
        if not last:
            for copy in halo_copies(sweep + 1):
                copy.start()

    for sweep in range(SWEEPS):
        for copy in halo_copies(sweep):
            copy.wait_send()
    cross_copy().wait_send()

    @pl.when(is_lead[1])
    def _():
        chip_cross_copy().wait_send()

    for d in range(2):
        map_copy(d).wait_send()

        @pl.when(jnp.logical_and(is_lead[d], jnp.logical_not(is_first[d])))
        def _():
            lead_map_copy(d).wait_send()

        for sweep in range(SWEEPS):
            tip_copy(sweep, d).wait_send()
            start_copy(sweep, d).wait_send()

            @pl.when(is_lead[d])
            def _():
                lead_copy(sweep, d).wait_send()

            @pl.when(jnp.logical_and(jnp.logical_not(is_lead[d]), jnp.logical_not(is_last[d])))
            def _():
                pair_copy(sweep, d, 0).wait_send()
                pair_copy(sweep, d, 1).wait_send()


def on_device(
    girth_size,
    wall_size,
    adjoint_start,
    right_side,
    pivot_inverse,
    lower_coupling,
    upper_coupling,
    girth_coeff,
    stream_coeff,
):
    nv, girth, wall, stream = adjoint_start.shape
    half = girth // HALVES
    flat = (nv, girth * wall, stream)
    blocks = (nv, nv, girth, wall, stream)
    tip = (nv, half, stream)
    half_blocks = (nv, nv, half, stream)
    dma = pltpu.SemaphoreType.DMA
    out = pl.pallas_call(
        functools.partial(kernel, girth_size, wall_size, (nv, girth, wall, stream)),
        out_shape=jax.ShapeDtypeStruct((nv, girth, wall, stream), F32),
        in_specs=[pl.BlockSpec(memory_space=pl.ANY)] * 7,
        out_specs=pl.BlockSpec(memory_space=pltpu.VMEM),
        scratch_shapes=[
            pltpu.VMEM((SWEEPS, nv, (girth + 2 * HALO) * wall, stream), F32),
            pltpu.VMEM((nv, girth, wall, stream), F32),
            pltpu.VMEM(blocks, jnp.bfloat16),
            pltpu.VMEM(blocks, jnp.bfloat16),
            pltpu.VMEM(blocks, jnp.bfloat16),
            pltpu.VMEM((nv, girth, wall, stream), jnp.bfloat16),
            pltpu.VMEM((nv, girth, wall, stream), jnp.bfloat16),
            pltpu.VMEM((2, nv, nv, wall, girth, stream), F32),
            pltpu.VMEM((nv, wall, girth, stream), F32),
            pltpu.VMEM((nv, girth, wall, stream), F32),
            pltpu.VMEM((2, *half_blocks), F32),
            pltpu.VMEM((2, 2, *half_blocks), F32),
            pltpu.VMEM((2, 2, *half_blocks), F32),
            pltpu.VMEM((nv, nv, wall, girth, stream), F32),
            pltpu.VMEM(half_blocks, F32),
            pltpu.VMEM((2, *half_blocks), F32),
            pltpu.VMEM((2, *half_blocks), F32),
            pltpu.VMEM((nv, wall, girth, stream), F32),
            pltpu.VMEM((SWEEPS, 2, *tip), F32),
            pltpu.VMEM((SWEEPS, 2, 2, *tip), F32),
            pltpu.VMEM((SWEEPS, 2, 2, *tip), F32),
            pltpu.VMEM((SWEEPS, 2, *tip), F32),
            pltpu.VMEM((SWEEPS, 2, *tip), F32),
            pltpu.VMEM((SWEEPS, 2, 2, *tip), F32),
            pltpu.VMEM((SWEEPS, 2, *tip), F32),
            pltpu.VMEM((nv, girth, stream), F32),
            pltpu.VMEM((nv, girth, stream), F32),
            pltpu.VMEM(tip, F32),
            pltpu.VMEM(tip, F32),
            dma((7,)),
            dma((SWEEPS, 2)),
            dma((SWEEPS, 2)),
            dma((2,)),
            dma((2,)),
            dma((2,)),
            dma((2,)),
            dma,
            dma,
            dma,
            dma,
            dma((SWEEPS, 2)),
            dma((SWEEPS, 2)),
            dma((SWEEPS, 2)),
            dma((SWEEPS, 2)),
            dma((SWEEPS, 2, 2)),
            dma((SWEEPS, 2)),
            dma((SWEEPS, 2)),
            dma((SWEEPS, 2)),
        ],
        compiler_params=pltpu.CompilerParams(
            collective_id=0, has_side_effects=True, vmem_limit_bytes=62 * 2**20
        ),
    )(
        adjoint_start.reshape(flat),
        right_side,
        pivot_inverse,
        lower_coupling,
        upper_coupling,
        girth_coeff,
        stream_coeff,
    )
    return out


def solution(mesh):
    in_specs = (
        P(None, "girth", "wall", None),
        P(None, "girth", "wall", None),
        P(None, None, "girth", "wall", None),
        P(None, None, "girth", "wall", None),
        P(None, None, "girth", "wall", None),
        P(None, "girth", "wall", None),
        P(None, "girth", "wall", None),
    )
    out_specs = P(None, "girth", "wall", None)
    return jax.shard_map(
        functools.partial(on_device, mesh.shape["girth"], mesh.shape["wall"]),
        mesh=mesh,
        in_specs=in_specs,
        out_specs=out_specs,
        check_vma=False,
    )
```
